128 devices in a mesh: seq: 16 (over y_lo, x, core), fsdp: 8 (over y_hi, z).
Axes of the slice: x: 4, y: 4 (y_hi: 2, y_lo: 2; y = y_hi * 2 + y_lo), z: 4, core: 2. Of those that a mesh axis runs over, the one named last changes fastest.
Arguments:
- inputs: bfloat16 [8, 2048, 1024], P('fsdp', 'seq'), may hold values from -6 to 6
- cotangent: bfloat16 [8, 2048, 1024], P('fsdp', 'seq'), may hold values from -6 to 6
- lengths: int32 [8], P('fsdp'), may hold values from 512 to 2048, as said below
- mixer_gain: bfloat16 [1024], P('fsdp'), may hold values from 0.099609375 to 1.8984375
- mixer_input: bfloat16 [1024, 1024], P('fsdp'), may hold values from -0.1875 to 0.1875
- mixer_gate: bfloat16 [1024, 1024], P('fsdp'), may hold values from -0.1875 to 0.1875
- mixer_kernel: bfloat16 [3, 1024], P(None, 'fsdp'), may hold values from -3.5 to 3.5
- lower_gain: bfloat16 [1024], P('fsdp'), may hold values from 0.099609375 to 1.8984375
- lower_gate: bfloat16 [1024, 2048], P('fsdp'), may hold values from -0.1875 to 0.1875
- lower_up: bfloat16 [1024, 2048], P('fsdp'), may hold values from -0.1875 to 0.1875
- lower_down: bfloat16 [2048, 1024], P('fsdp'), may hold values from -0.125 to 0.125
- attention_gain: bfloat16 [1024], P('fsdp'), may hold values from 0.099609375 to 1.8984375
- attention_query: bfloat16 [1024, 1024], P('fsdp'), may hold values from -0.1875 to 0.1875
- attention_key: bfloat16 [1024, 1024], P('fsdp'), may hold values from -0.1875 to 0.1875
- attention_value: bfloat16 [1024, 1024], P('fsdp'), may hold values from -0.1875 to 0.1875
- attention_output: bfloat16 [1024, 1024], P('fsdp'), may hold values from -0.75 to 0.75
- upper_gain: bfloat16 [1024], P('fsdp'), may hold values from 0.099609375 to 1.8984375
- upper_gate: bfloat16 [1024, 2048], P('fsdp'), may hold values from -0.1875 to 0.1875
- upper_up: bfloat16 [1024, 2048], P('fsdp'), may hold values from -0.1875 to 0.1875
- upper_down: bfloat16 [2048, 1024], P('fsdp'), may hold values from -0.125 to 0.125
Outputs:
- outputs: bfloat16 [8, 2048, 1024], P('fsdp', 'seq')
- input_grad: float32 [8, 2048, 1024], P('fsdp', 'seq')
- grad_mixer_gain: float32 [1024], P('fsdp')
- grad_mixer_input: float32 [1024, 1024], P('fsdp')
- grad_mixer_gate: float32 [1024, 1024], P('fsdp')
- grad_mixer_kernel: float32 [3, 1024], P(None, 'fsdp')
- grad_lower_gain: float32 [1024], P('fsdp')
- grad_lower_gate: float32 [1024, 2048], P('fsdp')
- grad_lower_up: float32 [1024, 2048], P('fsdp')
- grad_lower_down: float32 [2048, 1024], P('fsdp')
- grad_attention_gain: float32 [1024], P('fsdp')
- grad_attention_query: float32 [1024, 1024], P('fsdp')
- grad_attention_key: float32 [1024, 1024], P('fsdp')
- grad_attention_value: float32 [1024, 1024], P('fsdp')
- grad_attention_output: float32 [1024, 1024], P('fsdp')
- grad_upper_gain: float32 [1024], P('fsdp')
- grad_upper_gate: float32 [1024, 2048], P('fsdp')
- grad_upper_up: float32 [1024, 2048], P('fsdp')
- grad_upper_down: float32 [2048, 1024], P('fsdp')
The draws below stay inside these ranges and needn't reach their ends.
Inputs may be any that keep to these rules, and one draw needn't show every extreme that they name: lengths[s] is the number of valid slots of sequence s; its slots from lengths[s] on are padding. At least one sequence fills all 2048 slots.
All inputs are finite; a program needn't handle non-finite values.
Results may differ from the reference program's by a relative error of at most 0.025.
Values may be sent and summed in bfloat16 or wider, within the bound.
No kernel may reach another device: no remote copies, remote signals or barrier semaphores. Data moves between devices by JAX's collectives and lax.ppermute only.
A program may use at most 192 MiB of HBM per device.

```python
import jax
import jax.numpy as jnp
from jax import lax

D = 1024
FF = 2048
HEADS = 16
HEAD_DIM = 64
WINDOW = 64
SLOTS = 2048
SEQS = 8


def draw_lengths(key, part):
    key = jax.random.fold_in(key, 7)
    first_key, second_key = jax.random.split(key)
    drawn = jax.random.randint(first_key, (SEQS,), SLOTS // 4, SLOTS + 1)
    filled = jax.random.randint(second_key, (), 0, SEQS)
    return jnp.where(jnp.arange(SEQS) == filled, SLOTS, drawn).astype(jnp.int32)


def block_scale(key, shape, shards, least, top_value):
    level, own = 1.0, jax.random.fold_in(key, 6)
    for dim, parts in shards:
        steps = jnp.exp(jax.random.uniform(jax.random.fold_in(own, dim), (parts,), jnp.float32, least / len(shards), top_value / len(shards)))
        level = level * jnp.repeat(steps, shape[dim] // parts).reshape([-1 if axis == dim else 1 for axis in range(len(shape))])
    return level


def centred(rng, extent, spread, bound, cuts=(), held_as=jnp.bfloat16):
    level = block_scale(rng, extent, cuts, -0.22, 0.18) if cuts else 1.0
    entries = jax.random.normal(rng, extent, jnp.float32) * spread * level
    return jnp.minimum(jnp.maximum(entries, -bound), bound).astype(held_as)


def setup_inputs(seed: int = 0) -> dict:
    key_of = jax.random.split(jax.random.key(seed), 21)
    return {
        "inputs": centred(key_of[0], (SEQS, SLOTS, D), 1.0, 6.0, ((0, 8), (1, 16))),
        "cotangent": centred(key_of[1], (SEQS, SLOTS, D), 1.0, 6.0, ((0, 8), (1, 16))),
        "lengths": draw_lengths(jax.random.fold_in(key_of[20], 71), 0),
        "mixer_gain": jnp.clip(1.0 + 0.18 * jax.random.normal(key_of[3], (D,), jnp.float32), 0.099609375, 1.8984375).astype(jnp.bfloat16),
        "mixer_input": centred(key_of[4], (D, D), D ** -0.5, 0.1875, ((0, 8),)),
        "mixer_gate": centred(key_of[5], (D, D), D ** -0.5, 0.1875, ((0, 8),)),
        "mixer_kernel": centred(key_of[6], (3, D), 3 ** -0.5, 3.5, ((1, 8),)),
        "lower_gain": jnp.clip(1.0 + 0.18 * jax.random.normal(key_of[7], (D,), jnp.float32), 0.099609375, 1.8984375).astype(jnp.bfloat16),
        "lower_gate": centred(key_of[8], (D, FF), D ** -0.5, 0.1875, ((0, 8),)),
        "lower_up": centred(key_of[9], (D, FF), D ** -0.5, 0.1875, ((0, 8),)),
        "lower_down": centred(key_of[10], (FF, D), FF ** -0.5, 0.125, ((0, 8),)),
        "attention_gain": jnp.clip(1.0 + 0.18 * jax.random.normal(key_of[11], (D,), jnp.float32), 0.099609375, 1.8984375).astype(jnp.bfloat16),
        "attention_query": centred(key_of[12], (D, D), D ** -0.5, 0.1875, ((0, 8),)),
        "attention_key": centred(key_of[13], (D, D), D ** -0.5, 0.1875, ((0, 8),)),
        "attention_value": centred(key_of[14], (D, D), D ** -0.5, 0.1875, ((0, 8),)),
        "attention_output": centred(key_of[15], (D, D), (max(D // 32, WINDOW)) ** -0.5, 0.75, ((0, 8),)),
        "upper_gain": jnp.clip(1.0 + 0.18 * jax.random.normal(key_of[16], (D,), jnp.float32), 0.099609375, 1.8984375).astype(jnp.bfloat16),
        "upper_gate": centred(key_of[17], (D, FF), D ** -0.5, 0.1875, ((0, 8),)),
        "upper_up": centred(key_of[18], (D, FF), D ** -0.5, 0.1875, ((0, 8),)),
        "upper_down": centred(key_of[19], (FF, D), FF ** -0.5, 0.125, ((0, 8),)),
    }


@jax.custom_vjp
def low(v):
    return lax.optimization_barrier(v.astype(jnp.bfloat16)).astype(jnp.float32)

@jax.custom_vjp
def low_back(v):
    return v

def low_keep(v):
    return (low(v), None)

def low_pass(kept, grad):
    return (grad,)

def back_keep(v):
    return (v, None)

def back_low(kept, grad):
    return (low(grad),)
low.defvjp(low_keep, low_pass)
low_back.defvjp(back_keep, back_low)
EPSILON = 1e-05
MASKED_SCORE = -1e+30
PRECISE = lax.Precision.HIGHEST

def product(left, right):
    return jnp.dot(left, right, precision=PRECISE, preferred_element_type=jnp.float32)

def normalize(stream, norm_gain):
    row_scale = lax.rsqrt(lax.optimization_barrier(jnp.mean(stream * stream, axis=-1, keepdims=True)) + EPSILON)
    return stream * row_scale * norm_gain

def conv_mixer(stream, norm_gain, input_matrix, gate_matrix, kernel):
    normed = low(normalize(stream, norm_gain))
    signal = low_back(low(product(normed, input_matrix)))
    gate_act = low_back(product(normed, gate_matrix))
    padded = jnp.concatenate([jnp.zeros((2, signal.shape[1]), signal.dtype), signal], axis=0)
    conv_out = kernel[0] * signal + kernel[1] * padded[1:-1] + kernel[2] * padded[:-2]
    return stream + conv_out * gate_act

def swiglu(stream, norm_gain, gate_matrix, up_matrix, down_matrix):
    normed = low(normalize(stream, norm_gain))
    gate_act = low_back(product(normed, gate_matrix))
    upward = low_back(product(normed, up_matrix))
    hidden = low(jax.nn.silu(gate_act) * upward)
    return stream + low_back(product(hidden, down_matrix))

def attention(stream, norm_gain, query_matrix, key_matrix, value_matrix, output_matrix):
    slot_count = stream.shape[0]
    normed = low(normalize(stream, norm_gain))
    query = low_back(low(product(normed, query_matrix))).reshape(slot_count, HEADS, HEAD_DIM)
    keys = low_back(low(product(normed, key_matrix))).reshape(slot_count, HEADS, HEAD_DIM)
    values = low_back(low(product(normed, value_matrix))).reshape(slot_count, HEADS, HEAD_DIM)
    reach_rows = WINDOW - 1
    front = jnp.zeros((reach_rows, HEADS, HEAD_DIM), keys.dtype)
    keys_ext = jnp.concatenate([front, keys], axis=0)
    values_ext = jnp.concatenate([front, values], axis=0)
    block_rows = min(slot_count, 512)

    def one_block(block_start):
        query_piece = lax.dynamic_slice_in_dim(query, block_start, block_rows, 0)
        key_piece = lax.dynamic_slice_in_dim(keys_ext, block_start, block_rows + reach_rows, 0)
        value_piece = lax.dynamic_slice_in_dim(values_ext, block_start, block_rows + reach_rows, 0)
        scores = jnp.einsum('qhd,khd->hqk', query_piece, key_piece, precision=PRECISE) * HEAD_DIM ** (-0.5)
        scores = low_back(scores)
        query_place = block_start + jnp.arange(block_rows)
        key_place = block_start - reach_rows + jnp.arange(block_rows + reach_rows)
        allowed = (key_place[None, :] <= query_place[:, None]) & (key_place[None, :] > query_place[:, None] - WINDOW) & (key_place[None, :] >= 0)
        scores = jnp.where(allowed[None], scores, MASKED_SCORE)
        probability = low(jax.nn.softmax(scores, axis=-1))
        return jnp.einsum('hqk,khd->qhd', probability, value_piece, precision=PRECISE)
    starts = (jnp.arange(slot_count // block_rows) * block_rows).astype(jnp.int32)
    blocks = lax.map(jax.checkpoint(one_block), starts)
    attended = low_back(low(blocks.reshape(slot_count, HEADS * HEAD_DIM)))
    return stream + low_back(product(attended, output_matrix))

def layers(stream, weights):
    mixer_gain, mixer_input, mixer_gate, mixer_kernel, lower_gain, lower_gate, lower_up, lower_down, attention_gain, attention_query, attention_key, attention_value, attention_output, upper_gain, upper_gate, upper_up, upper_down = weights
    stream = conv_mixer(stream, mixer_gain, mixer_input, mixer_gate, mixer_kernel)
    stream = swiglu(stream, lower_gain, lower_gate, lower_up, lower_down)
    stream = attention(stream, attention_gain, attention_query, attention_key, attention_value, attention_output)
    return swiglu(stream, upper_gain, upper_gate, upper_up, upper_down)

def reference(inputs, cotangent, lengths, mixer_gain, mixer_input, mixer_gate, mixer_kernel, lower_gain, lower_gate, lower_up, lower_down, attention_gain, attention_query, attention_key, attention_value, attention_output, upper_gain, upper_gate, upper_up, upper_down):
    raw = (mixer_gain, mixer_input, mixer_gate, mixer_kernel, lower_gain, lower_gate, lower_up, lower_down, attention_gain, attention_query, attention_key, attention_value, attention_output, upper_gain, upper_gate, upper_up, upper_down)
    weights = tuple((item.astype(jnp.float32) for item in raw))

    def one_sequence(totals, sequence_item):
        seq_input, seq_cot, seq_length = sequence_item
        start_stream = seq_input.astype(jnp.float32)
        result, pullback = jax.vjp(layers, start_stream, weights)
        valid = (jnp.arange(SLOTS) < seq_length).astype(jnp.float32)
        grad_input, grad_weights = pullback(seq_cot.astype(jnp.float32) * valid[:, None])
        totals = jax.tree.map(lambda first, second: first + second, totals, grad_weights)
        return (totals, (result.astype(jnp.bfloat16), grad_input))
    zeros = jax.tree.map(jnp.zeros_like, weights)
    totals, (outputs, input_grad) = lax.scan(one_sequence, zeros, (inputs, cotangent, lengths))
    return (outputs, input_grad, totals[0], totals[1], totals[2], totals[3], totals[4], totals[5], totals[6], totals[7], totals[8], totals[9], totals[10], totals[11], totals[12], totals[13], totals[14], totals[15], totals[16])
```

```python
import functools

import jax
import jax.numpy as jnp
from jax import lax
from jax.experimental import pallas as pl
from jax.experimental.pallas import tpu as pltpu
from jax.sharding import Mesh
from jax.sharding import PartitionSpec as P

EPSILON = 1e-05
MASKED = -1e30
AXES = ("yl", "x", "c", "yh", "z")
SIZES = (2, 4, 2, 2, 4)
F32 = jnp.float32
BF16 = jnp.bfloat16
ROWS = 128
PAIR = 256
D = 1024
HALF = 512
REACH = 64
SCALE = 64 ** (-0.5)


def at(axis):
    return lax.axis_index(axis)


def swap_core(value):
    return lax.ppermute(value, "c", [(0, 1), (1, 0)])


def hop_z(value):
    pairs = [(c * 4 + z, c * 4 + (z + 1 - 2 * c) % 4) for c in range(2) for z in range(4)]
    return lax.ppermute(value, ("c", "z"), pairs)


def cross(value):
    return lax.ppermute(value, ("yl", "yh"), [(0, 3), (3, 0), (1, 2), (2, 1)])


def swap_yl(value):
    return lax.ppermute(value, "yl", [(0, 1), (1, 0)])


def chip_shift(value, by):
    pairs = [(i, i + by) for i in range(8) if 0 <= i + by < 8]
    return lax.ppermute(value, ("yl", "x"), pairs)


def spread(value, axes, count):
    return lax.all_to_all(
        jnp.broadcast_to(value[None], (count,) + value.shape), axes, 0, 0, tiled=True
    )


def tie(values, after):
    out = lax.optimization_barrier(tuple(values) + tuple(after))
    return out[: len(values)]


def both_cores(own, other, axis=0):
    first = at("c") == 0
    return jnp.concatenate(
        [jnp.where(first, own, other), jnp.where(first, other, own)], axis=axis
    )


def gather_slabs(slabs):
    yl = at("yl")
    state = [dict(own=[s], got=[], rest=[]) for s in slabs]
    previous = ()
    for step in range(4 * len(slabs) + 1):
        wants = []
        for g, st in enumerate(state):
            k = step - 4 * g
            if 0 <= k < 3:
                wants.append((hop_z, st["own"], st["own"][k]))
            if 0 <= k < 4:
                half = lax.dynamic_index_in_dim(st["own"][k], 1 - yl, 0, keepdims=False)
                wants.append((cross, st["got"], half))
            if 1 <= k < 5:
                wants.append((swap_yl, st["rest"], st["got"][k - 1]))
        values = tie([w[2] for w in wants], previous)
        previous = [w[0](v) for w, v in zip(wants, values)]
        for w, v in zip(wants, previous):
            w[1].append(v)
    return state


def assemble_kernel(plan, count, place, *refs):
    own, got, rest = refs[0:4], refs[4:8], refs[8:12]
    outs = refs[12:-1]
    sems = refs[-1]
    copies = []

    def put(source, f, half):
        for take, out, dest in plan:
            copies.append(
                pltpu.make_async_copy(take(source), dest(outs[out], f, half), sems.at[len(copies)])
            )

    yl = place[8]
    for s in range(4):
        for half in range(2):
            put(own[s].at[half], place[s], half)
        put(got[s], place[4 + s], yl)
        put(rest[s], place[4 + s], 1 - yl)
    assert len(copies) == count
    for copy in copies:
        copy.start()
    for copy in copies:
        copy.wait()


def assemble(pieces, plan, shapes, place):
    count = 16 * len(plan)
    return pl.pallas_call(
        functools.partial(assemble_kernel, plan, count),
        out_shape=[jax.ShapeDtypeStruct(s, BF16) for s in shapes],
        in_specs=[pl.BlockSpec(memory_space=pltpu.SMEM)] + [pl.BlockSpec(memory_space=pl.ANY)] * 12,
        out_specs=[pl.BlockSpec(memory_space=pl.ANY)] * len(shapes),
        scratch_shapes=[pltpu.SemaphoreType.DMA((count,))],
        name="assemble",
    )(place, *pieces["own"], *pieces["got"], *pieces["rest"])


def rows_of(half, size=64):
    return pl.ds(half * size, size)


MIXER_PLAN = [
    (lambda s: s.at[0:64], 0, lambda o, f, h: o.at[f, rows_of(h)]),
    (lambda s: s.at[64:80], 1, lambda o, f, h: o.at[f, h]),
]
FEED_PLAN = [
    (lambda s: s.at[0], 0, lambda o, f, h: o.at[f, rows_of(h), 0:1024]),
    (lambda s: s.at[1], 0, lambda o, f, h: o.at[f, rows_of(h), 1024:2048]),
    (lambda s: s.at[2], 1, lambda o, f, h: o.at[f, rows_of(h)]),
]
HEAD_PLAN = [
    (lambda s: s.at[0], 0, lambda o, f, h: o.at[f, rows_of(h), 0:1024]),
    (lambda s: s.at[1, :, 0:512], 0, lambda o, f, h: o.at[f, rows_of(h), 1024:1536]),
    (lambda s: s.at[1, :, 512:1024], 1, lambda o, f, h: o.at[f, h]),
]


def dot(left, right, dims=((1,), (0,))):
    return lax.dot_general(left, right, (dims, ((), ())), preferred_element_type=F32)


def dot_t(left, right):
    return dot(left, right, ((1,), (1,)))


def t_dot(left, right):
    return dot(left, right, ((0,), (0,)))


def normalize(stream, gain):
    scale = lax.rsqrt(jnp.mean(stream * stream, axis=-1, keepdims=True) + EPSILON)
    return (stream * scale * gain).astype(BF16), scale


def norm_back(stream, scale, gain, upstream):
    weighted = upstream * gain
    inner = jnp.mean(weighted * stream, axis=-1, keepdims=True)
    grad = scale * (weighted - stream * scale * scale * inner)
    return grad, jnp.sum(upstream * stream * scale, axis=0)


def add_cores(partial):
    return partial + swap_core(partial.astype(BF16)).astype(F32)


def lane_mask(shape, head):
    lane = lax.broadcasted_iota(jnp.int32, shape, 1)
    return (lane // 64) == head


def window_mask(block, first):
    i = lax.broadcasted_iota(jnp.int32, (128, 192), 0)
    j = lax.broadcasted_iota(jnp.int32, (128, 192), 1)
    allowed = (j > i) & (j <= i + REACH)
    if block == 0:
        allowed = allowed & ((j >= REACH) | (first == 0))
    return allowed


def probabilities(q, k, allowed):
    scores = jnp.where(allowed, dot_t(q, k) * SCALE, MASKED)
    weights = jnp.exp(scores - jnp.max(scores, axis=-1, keepdims=True))
    return weights / jnp.sum(weights, axis=-1, keepdims=True)


def attend_kernel(first_ref, q_ref, k_ref, v_ref, o_ref):
    for block in range(2):
        allowed = window_mask(block, first_ref[0])
        rows, keys = pl.ds(block * 128, 128), pl.ds(block * 128, 192)
        for pair in range(4):
            cols = pl.ds(pair * 128, 128)
            q, k, v = q_ref[rows, cols], k_ref[keys, cols], v_ref[keys, cols]
            outs = []
            for head in range(2):
                q_head = jnp.where(lane_mask(q.shape, head), q, jnp.zeros_like(q))
                p = probabilities(q_head, k, allowed)
                outs.append(dot(p.astype(BF16), v))
            o_ref[rows, cols] = jnp.where(lane_mask(q.shape, 0), outs[0], outs[1]).astype(BF16)


def attend(first, q, k_ext, v_ext):
    return pl.pallas_call(
        attend_kernel,
        out_shape=jax.ShapeDtypeStruct((PAIR, HALF), BF16),
        in_specs=[pl.BlockSpec(memory_space=pltpu.SMEM)]
        + [pl.BlockSpec(memory_space=pltpu.VMEM)] * 3,
        out_specs=pl.BlockSpec(memory_space=pltpu.VMEM),
        name="attend",
    )(first, q, k_ext, v_ext)


def attend_back_kernel(first_ref, q_ref, k_ref, v_ref, ep_ref, eq_ref, ek_ref, ev_ref):
    for pair in range(4):
        cols = pl.ds(pair * 128, 128)
        eks, evs = [], []
        for block in range(2):
            allowed = window_mask(block, first_ref[0])
            rows, keys = pl.ds(block * 128, 128), pl.ds(block * 128, 192)
            q, k, v = q_ref[rows, cols], k_ref[keys, cols], v_ref[keys, cols]
            ep = ep_ref[rows, cols]
            eq_out, ek_out, ev_out = [], [], []
            for head in range(2):
                own = lane_mask(q.shape, head)
                p = probabilities(jnp.where(own, q, jnp.zeros_like(q)), k, allowed)
                dp = dot_t(jnp.where(own, ep, jnp.zeros_like(ep)), v)
                inner = jnp.sum(p * dp, axis=-1, keepdims=True)
                es = (p * (dp - inner)).astype(BF16)
                ev_out.append(t_dot(p.astype(BF16), ep))
                ek_out.append(t_dot(es, q))
                eq_out.append(dot(es, k))
            pick_q = lane_mask((128, 128), 0)
            pick_k = lane_mask((192, 128), 0)
            eq_ref[rows, cols] = (jnp.where(pick_q, eq_out[0], eq_out[1]) * SCALE).astype(BF16)
            eks.append(jnp.where(pick_k, ek_out[0], ek_out[1]) * SCALE)
            evs.append(jnp.where(pick_k, ev_out[0], ev_out[1]))
        for parts, ref in ((eks, ek_ref), (evs, ev_ref)):
            ref[pl.ds(0, 128), cols] = parts[0][:128]
            ref[pl.ds(128, 64), cols] = parts[0][128:] + parts[1][:64]
            ref[pl.ds(192, 128), cols] = parts[1][64:]


def attend_back(first, q, k_ext, v_ext, ep):
    return pl.pallas_call(
        attend_back_kernel,
        out_shape=[
            jax.ShapeDtypeStruct((PAIR, HALF), BF16),
            jax.ShapeDtypeStruct((PAIR + REACH, HALF), F32),
            jax.ShapeDtypeStruct((PAIR + REACH, HALF), F32),
        ],
        in_specs=[pl.BlockSpec(memory_space=pltpu.SMEM)]
        + [pl.BlockSpec(memory_space=pltpu.VMEM)] * 4,
        out_specs=[pl.BlockSpec(memory_space=pltpu.VMEM)] * 3,
        name="attend_back",
    )(first, q, k_ext, v_ext, ep)


def own_rows(value):
    return lax.dynamic_slice_in_dim(value, at("c") * ROWS, ROWS, 0)


def share_inputs(normed, hidden):
    own = own_rows(normed)
    if hidden is None:
        packed = own
    else:
        packed = jnp.concatenate([own, hidden.reshape(-1, D)], axis=0)
    got = spread(packed, "x", 4).reshape(4, -1, D)
    half = got[:, :ROWS]
    other = swap_core(half)
    all_normed = both_cores(half, other, axis=1).reshape(4 * PAIR, D)
    if hidden is None:
        return all_normed, None
    return all_normed, got[:, ROWS:].reshape(4 * PAIR, hidden.shape[1])


def share_grads(parts):
    quarters = [p.reshape(PAIR, 4, -1).transpose(1, 0, 2) for p in parts]
    packed = jnp.concatenate(quarters, axis=2)
    return lax.all_to_all(packed, "x", 0, 0, tiled=True).reshape(4 * PAIR, -1)


def settle(parts, extra=None):
    width = sum(p.shape[1] for p in parts)
    packed = jnp.concatenate([p.astype(BF16) for p in parts], axis=1)
    packed = packed.reshape(8, 2, 64, width).transpose(1, 0, 2, 3)
    if extra is not None:
        extra = jnp.pad(extra.astype(BF16), ((0, 0), (0, 16 - extra.shape[1]), (0, width - 128)))
        extra = jnp.broadcast_to(extra[None], (2,) + extra.shape)
        packed = jnp.concatenate([packed, extra], axis=2)
    rows = packed.shape[2]
    got = lax.all_to_all(packed.reshape(16, rows, width), ("yl", "yh", "z"), 0, 0, tiled=True)
    total = jnp.sum(got.astype(F32), axis=0).astype(BF16)
    return spread(total, ("yl", "x", "c"), 16).reshape(2, 4, 2, rows, width)


def body(
    inputs,
    cotangent,
    lengths,
    mixer_gain,
    mixer_input,
    mixer_gate,
    mixer_kernel,
    lower_gain,
    lower_gate,
    lower_up,
    lower_down,
    attention_gain,
    attention_query,
    attention_key,
    attention_value,
    attention_output,
    upper_gain,
    upper_gate,
    upper_up,
    upper_down,
):
    c, x, yl, yh, z = at("c"), at("x"), at("yl"), at("yh"), at("z")
    chip = yl * 4 + x
    first_chip = (chip == 0).astype(jnp.int32).reshape(1)

    def half_cols(matrix):
        return lax.dynamic_slice_in_dim(matrix, c * HALF, HALF, 1)

    def block_cols(matrix, width):
        blocks = matrix.reshape(ROWS, 8, 2, width)
        return lax.dynamic_index_in_dim(blocks, c, 2, keepdims=False).reshape(ROWS, 8 * width)

    small = jnp.concatenate(
        [
            mixer_gain[None],
            lower_gain[None],
            attention_gain[None],
            upper_gain[None],
            mixer_kernel,
            jnp.zeros((9, ROWS), BF16),
        ],
        axis=0,
    )
    small = jnp.pad(small, ((0, 0), (0, D - ROWS)))
    mixer_own = jnp.concatenate([half_cols(mixer_input), half_cols(mixer_gate)], axis=1)
    mixer_slab = jnp.concatenate(
        [mixer_own.reshape(2, 64, D), jnp.broadcast_to(small[None], (2, 16, D))], axis=1
    )

    def feed_slab(gate, up, down):
        parts = [
            block_cols(gate, ROWS),
            block_cols(up, ROWS),
            lax.dynamic_slice_in_dim(down, c * ROWS, ROWS, 0),
        ]
        return jnp.stack([p.reshape(2, 64, D) for p in parts], axis=1)

    wo = lax.dynamic_slice_in_dim(attention_output, c * 64, 64, 0)
    qk = jnp.concatenate([block_cols(attention_query, 64), block_cols(attention_key, 64)], axis=1)
    vw = jnp.concatenate(
        [
            block_cols(attention_value, 64).reshape(2, 64, HALF),
            wo.reshape(64, 2, HALF).transpose(1, 0, 2),
        ],
        axis=2,
    )
    head_slab = jnp.stack([qk.reshape(2, 64, D), vw], axis=1)

    pieces = gather_slabs(
        [
            mixer_slab,
            feed_slab(lower_gate, lower_up, lower_down),
            head_slab,
            feed_slab(upper_gate, upper_up, upper_down),
        ]
    )
    zs = [jnp.mod(z - (1 - 2 * c) * s, 4) for s in range(4)]
    place = jnp.stack([yh * 4 + v for v in zs] + [(1 - yh) * 4 + v for v in zs] + [yl]).astype(
        jnp.int32
    )
    mix_w, small_all = assemble(pieces[0], MIXER_PLAN, [(8, 128, D), (8, 2, 16, D)], place)
    mix_w = mix_w.reshape(D, D)
    small_all = small_all[:, 0, :, :ROWS].transpose(1, 0, 2).reshape(16, D).astype(F32)
    gain_m, gain_l, gain_a, gain_u = (small_all[i] for i in range(4))
    taps = lax.dynamic_slice_in_dim(small_all[4:7], c * HALF, HALF, 1)

    mine = jnp.concatenate([inputs[0], cotangent[0]], axis=1)
    two = both_cores(mine, swap_core(mine))
    start = two[:, :D].astype(F32)
    place_row = chip * PAIR + jnp.arange(PAIR, dtype=jnp.int32)
    valid = (place_row < lengths[0]).astype(F32)
    e4 = two[:, D:].astype(F32) * valid[:, None]

    halo = chip_shift(two[PAIR - 16 :, :D], 1)
    with_halo = jnp.concatenate([halo.astype(F32), start], axis=0)
    na_ext, _ = normalize(with_halo, gain_m)
    na = na_ext[16:]
    scale_a = lax.rsqrt(jnp.mean(start * start, axis=-1, keepdims=True) + EPSILON)
    both = dot(na_ext, mix_w)
    signal = both[:, :HALF].astype(BF16).astype(F32)
    gate = both[16:, HALF:]
    shifted = [signal[16:], signal[15:-1], signal[14:-2]]
    conv = sum(taps[m] * shifted[m] for m in range(3))
    mixed = conv * gate
    h1 = start + both_cores(mixed, swap_core(mixed.astype(BF16)).astype(F32), axis=1)

    def feed(stream, gain, weights):
        w_in, w_out = weights
        normed, scale = normalize(stream, gain)
        act = dot(normed, w_in)
        hidden = (jax.nn.silu(act[:, :D]) * act[:, D:]).astype(BF16)
        return normed, scale, act, hidden, dot(hidden, w_out)

    def feed_weights(k):
        w_in, w_out = assemble(pieces[k], FEED_PLAN, [(8, 128, 2 * D), (8, 128, D)], place)
        return w_in.reshape(D, 2 * D), w_out.reshape(D, D)

    lower_w = feed_weights(1)
    nb, scale_b, act_l, ha, part = feed(h1, gain_l, lower_w)
    h2 = h1 + add_cores(part)

    qkv_w, out_w = assemble(pieces[2], HEAD_PLAN, [(8, 128, 3 * HALF), (8, 2, 64, HALF)], place)
    qkv_w = qkv_w.reshape(D, 3 * HALF)
    out_w = out_w.transpose(0, 2, 1, 3).reshape(HALF, D)
    nc, scale_c = normalize(h2, gain_a)
    qkv = dot(nc, qkv_w).astype(BF16)
    q = qkv[:, :HALF]
    edge = chip_shift(qkv[PAIR - REACH :, HALF:], 1)
    kv_ext = jnp.concatenate([edge, qkv[:, HALF:]], axis=0)
    k_ext, v_ext = kv_ext[:, :HALF], kv_ext[:, HALF:]
    o = attend(first_chip, q, k_ext, v_ext)
    h3 = h2 + add_cores(dot(o, out_w))

    upper_w = feed_weights(3)
    nd, scale_d, act_u, hb, part = feed(h3, gain_u, upper_w)
    other_part = lax.dynamic_slice_in_dim(part, (1 - c) * ROWS, ROWS, 0).astype(BF16)
    outputs = own_rows(h3) + own_rows(part) + swap_core(other_part).astype(F32)

    nd_all, hb_all = share_inputs(nd, hb)
    nb_all, ha_all = share_inputs(nb, ha)
    nc_all, o_all = share_inputs(nc, o)
    na_all, _ = share_inputs(na, None)

    def feed_back(stream, scale, gain, weights, act, grad_out, n_all, h_all):
        w_in, w_out = weights
        branch = grad_out.astype(BF16)
        grad_hidden = dot_t(branch, w_out)
        gate_act, up_act = act[:, :D], act[:, D:]
        sig = jax.nn.sigmoid(gate_act)
        grad_gate = (grad_hidden * up_act * sig * (1.0 + gate_act * (1.0 - sig))).astype(BF16)
        grad_up = (grad_hidden * gate_act * sig).astype(BF16)
        both_grads = jnp.concatenate([grad_gate, grad_up], axis=1)
        grad_normed = add_cores(dot_t(both_grads, w_in))
        grad_stream, grad_gain = norm_back(stream, scale, gain, grad_normed)
        shared = share_grads([grad_gate, grad_up, branch])
        done = settle([t_dot(n_all, shared[:, : D // 2]), t_dot(h_all, shared[:, D // 2 :])])
        return grad_out + grad_stream, grad_gain, done

    e3, gain_grad_u, done_u = feed_back(h3, scale_d, gain_u, upper_w, act_u, e4, nd_all, hb_all)

    eo = e3.astype(BF16)
    ep = dot_t(eo, out_w).astype(BF16)
    eq, ek_ext, ev_ext = attend_back(first_chip, q, k_ext, v_ext, ep)
    ekv_edge = jnp.concatenate([ek_ext[:REACH], ev_ext[:REACH]], axis=1).astype(BF16)
    back = chip_shift(ekv_edge, -1).astype(F32)
    ekv = jnp.concatenate([ek_ext[REACH:], ev_ext[REACH:]], axis=1)
    ekv = jnp.concatenate([ekv[: PAIR - REACH], ekv[PAIR - REACH :] + back], axis=0).astype(BF16)
    eqkv = jnp.concatenate([eq, ekv], axis=1)
    grad_nc = add_cores(dot_t(eqkv, qkv_w))
    grad_stream, gain_grad_a = norm_back(h2, scale_c, gain_a, grad_nc)
    e2 = e3 + grad_stream
    shared = share_grads([eq, ekv[:, :HALF], ekv[:, HALF:], eo])
    out_grad = t_dot(o_all, shared[:, 384:])
    out_grad = out_grad.reshape(8, 64, 2, 128).transpose(0, 2, 1, 3).reshape(D, 128)
    done_a = settle([t_dot(nc_all, shared[:, :384]), out_grad])

    e1, gain_grad_l, done_l = feed_back(h1, scale_b, gain_l, lower_w, act_l, e2, nb_all, ha_all)

    e1_own = lax.dynamic_slice_in_dim(e1, c * HALF, HALF, 1)
    egate = (e1_own * conv).astype(BF16)
    ec = e1_own * gate
    tap_grads = jnp.stack([jnp.sum(ec * shifted[m], axis=0) for m in range(3)])
    ec_next = chip_shift(ec[:8], -1)
    ec_ext = jnp.concatenate([ec, ec_next], axis=0)
    esig = sum(taps[m] * ec_ext[m : m + PAIR] for m in range(3)).astype(BF16)
    emix = jnp.concatenate([esig, egate], axis=1)
    grad_na = dot_t(emix, mix_w)
    other_na = lax.dynamic_slice_in_dim(grad_na, (1 - c) * ROWS, ROWS, 0).astype(BF16)
    grad_na = own_rows(grad_na) + swap_core(other_na).astype(F32)
    grad_start, gain_grad_m = norm_back(own_rows(start), own_rows(scale_a), gain_m, grad_na)
    input_grad = own_rows(e1) + grad_start
    shared = share_grads([esig, egate])
    once = (c == 0).astype(F32)
    wide_taps = lax.dynamic_update_slice(jnp.zeros((3, D), F32), tap_grads, (0, c * HALF))
    gains = jnp.stack([gain_grad_m, gain_grad_l * once, gain_grad_a * once, gain_grad_u * once])
    extra = jnp.concatenate([gains, wide_taps], axis=0).reshape(7, 8, ROWS).transpose(1, 0, 2)
    done_m = settle([t_dot(na_all, shared)], extra)

    def in_cols(part, width):
        part = part.reshape(2, 4, 2, 64, 2, width).transpose(0, 3, 1, 4, 2, 5)
        return part.reshape(ROWS, 16 * width).astype(F32)

    def feed_grads(done):
        down = done[..., 512:].transpose(2, 0, 3, 1, 4).reshape(2 * ROWS, D).astype(F32)
        return in_cols(done[..., :256], 128), in_cols(done[..., 256:512], 128), down

    def head_grads(done):
        out = done[..., 384:].transpose(2, 3, 1, 0, 4).reshape(ROWS, D).astype(F32)
        return [in_cols(done[..., 128 * i : 128 * i + 128], 64) for i in range(3)] + [out]

    def half_grads(part):
        return part.transpose(0, 3, 2, 1, 4).reshape(ROWS, D).astype(F32)

    tail = jnp.sum(done_m[0, :, :, 64:, :ROWS].astype(F32), axis=(0, 1))
    lower_grads, upper_grads, heads = feed_grads(done_l), feed_grads(done_u), head_grads(done_a)
    return (
        outputs.astype(BF16)[None],
        input_grad[None],
        tail[0],
        half_grads(done_m[:, :, :, :64, :128]),
        half_grads(done_m[:, :, :, :64, 128:]),
        tail[4:7],
        tail[1],
        *lower_grads,
        tail[2],
        *heads,
        tail[3],
        *upper_grads,
    )


def solution(mesh):
    fine = Mesh(mesh.devices.reshape(SIZES), AXES)
    rows = ("yh", "z")
    slots = P(rows, ("yl", "x", "c"), None)
    vector, matrix, columns = P(rows), P(rows, None), P(None, rows)
    weights = (
        (vector, matrix, matrix, columns)
        + (vector, matrix, matrix, matrix)
        + (vector, matrix, matrix, matrix, matrix)
        + (vector, matrix, matrix, matrix)
    )
    return jax.shard_map(
        body,
        mesh=fine,
        in_specs=(slots, slots, vector) + weights,
        out_specs=(slots, slots) + weights,
        check_vma=False,
    )
```

```python
import functools

import jax
import jax.numpy as jnp
from jax import lax
from jax.experimental import pallas as pl
from jax.experimental.pallas import tpu as pltpu
from jax.sharding import Mesh
from jax.sharding import PartitionSpec as P

EPSILON = 1e-05
MASKED = -1e30
AXES = ("yl", "x", "c", "yh", "z")
SIZES = (2, 4, 2, 2, 4)
SEQ = ("yl", "x", "c")
SUMS = ("yl", "yh", "z")
F32 = jnp.float32
BF16 = jnp.bfloat16
ROWS = 128
PAIR = 256
D = 1024
HALF = 512
REACH = 64
SCALE = 64 ** (-0.5)


def at(axis):
    return lax.axis_index(axis)


def swap_core(value):
    return lax.ppermute(value, "c", [(0, 1), (1, 0)])


def hop_z(value):
    pairs = [(c * 4 + z, c * 4 + (z + 1 - 2 * c) % 4) for c in range(2) for z in range(4)]
    return lax.ppermute(value, ("c", "z"), pairs)


def cross(value):
    return lax.ppermute(value, ("yl", "yh"), [(0, 3), (3, 0), (1, 2), (2, 1)])


def swap_yl(value):
    return lax.ppermute(value, "yl", [(0, 1), (1, 0)])


def chip_shift(value, by):
    pairs = [(i, i + by) for i in range(8) if 0 <= i + by < 8]
    return lax.ppermute(value, ("yl", "x"), pairs)


def along_x(value, by):
    return lax.ppermute(value, "x", [(i, (i + by) % 4) for i in range(4)])


def spread(value, axes, count):
    return lax.all_to_all(
        jnp.broadcast_to(value[None], (count,) + value.shape), axes, 0, 0, tiled=True
    )


def tie(values, after):
    out = lax.optimization_barrier(tuple(values) + tuple(after))
    return out[: len(values)]


def both_cores(own, other, axis=0):
    first = at("c") == 0
    return jnp.concatenate(
        [jnp.where(first, own, other), jnp.where(first, other, own)], axis=axis
    )


VMEM = pl.BlockSpec(memory_space=pltpu.VMEM)
SMEM = pl.BlockSpec(memory_space=pltpu.SMEM)
BIG = pltpu.CompilerParams(vmem_limit_bytes=40 * 1024 * 1024)


def in_lanes(shape, which, width):
    return lax.broadcasted_iota(jnp.int32, shape, 1) // width == which


def hidden_blocks(ref, rows, core):
    blocks = [
        ref[rows, pl.ds(pl.multiple_of(f * 256 + core * 128, 128), 128)].astype(F32)
        for f in range(8)
    ]
    for b in range(8):
        out = None
        for i in range(4):
            source = blocks[4 * (b % 2) + i]
            piece = pltpu.roll(source, (i - b // 2) % 4 * 32, 1)
            out = piece if out is None else jnp.where(in_lanes(piece.shape, i, 32), piece, out)
        yield b, out.astype(BF16)


def head_block(ref, rows, block, core):
    left = ref[rows, pl.ds(block * 256, 128)].astype(F32)
    right = ref[rows, pl.ds(block * 256 + 128, 128)].astype(F32)
    low = lax.broadcasted_iota(jnp.int32, left.shape, 1) < 64
    first = jnp.where(low, left, pltpu.roll(right, 64, 1))
    second = jnp.where(low, pltpu.roll(left, 64, 1), right)
    return jnp.where(core == 0, first, second).astype(BF16)


def first_slab_kernel(place, m_in, m_gate, small, gate, up, down, out):
    core = place[0]
    for half in range(2):
        rows = pl.ds(half * 64, 64)
        for i, ref in enumerate((m_in, m_gate)):
            out[half, 0:64, pl.ds(i * HALF, HALF)] = ref[
                rows, pl.ds(pl.multiple_of(core * HALF, HALF), HALF)
            ]
        out[half, 64:80, :] = jnp.zeros((16, D), BF16)
        out[half, 64:80, 0:128] = small[...]
        for start, ref in ((80, gate), (144, up)):
            for block, value in hidden_blocks(ref, rows, core):
                out[half, pl.ds(start, 64), pl.ds(block * 128, 128)] = value
        out[half, 208:272, :] = down[pl.ds(pl.multiple_of(core * 128 + half * 64, 64), 64), :]


def head_slab_kernel(place, q, k, v, wo, out):
    core = place[0]
    for half in range(2):
        rows = pl.ds(half * 64, 64)
        for block in range(4):
            out[half, 0:64, pl.ds(block * 128, 128)] = head_block(q, rows, block, core)
            out[half, 0:64, pl.ds(512 + block * 128, 128)] = head_block(k, rows, block, core)
            out[half, 64:128, pl.ds(block * 128, 128)] = head_block(v, rows, block, core)
        out[half, 64:128, 512:1024] = wo[
            pl.ds(pl.multiple_of(core * 64, 64), 64), pl.ds(half * HALF, HALF)
        ]


def upper_part_kernel(place, gate, up, down, out):
    core, part = place[0], place[1]
    rows = pl.ds(pl.multiple_of(part * 32, 32), 32)
    low = down[pl.ds(pl.multiple_of(core * 128 + part * 32, 32), 32), :]
    for copy in range(8):
        out[copy, 64:96, :] = low
    for start, ref in ((0, gate), (32, up)):
        for block, value in hidden_blocks(ref, rows, core):
            for copy in range(8):
                out[copy, pl.ds(start, 32), pl.ds(block * 128, 128)] = value


def build(kernel, shapes, place, *arrays, name):
    many = isinstance(shapes, list)
    return pl.pallas_call(
        kernel,
        out_shape=[jax.ShapeDtypeStruct(*s) for s in shapes]
        if many
        else jax.ShapeDtypeStruct(*shapes),
        in_specs=[SMEM] + [VMEM] * len(arrays),
        out_specs=[VMEM] * len(shapes) if many else VMEM,
        compiler_params=BIG,
        name=name,
    )(place, *arrays)


def gather_slabs(slabs, other):
    yl = at("yl")
    state = [dict(own=[s], got=[], rest=[]) for s in slabs]
    moved = []
    for step in range(4 * len(slabs) + 1):
        if moved:
            values = [st[key][-1] for st, key in moved]
            if step == 1:
                *values, other = tie([*values, other], [])
            else:
                values = tie(values, [])
            for (st, key), value in zip(moved, values):
                st[key][-1] = value
        moved, made = [], []
        for g, st in enumerate(state):
            k = step - 4 * g
            if 0 <= k < 3:
                made.append((st, "own", hop_z(st["own"][k])))
            if 1 <= k < 5:
                made.append((st, "rest", swap_yl(st["got"][k - 1])))
            if 0 <= k < 4:
                half = lax.dynamic_index_in_dim(st["own"][k], 1 - yl, 0, keepdims=False)
                made.append((st, "got", cross(half)))
        for st, key, value in made:
            st[key].append(value)
            moved.append((st, key))
    return state, other


def assemble_kernel(plan, place, *refs):
    own, got, rest = refs[0:4], refs[4:8], refs[8:12]
    outs = refs[12:]

    def put(source, f, half):
        for rows, cols, out, height, dest in plan:
            if height == 0:
                for i in range(2):
                    outs[out][half * 2 + i, f] = source[rows.start + i * 32 : rows.start + i * 32 + 32]
                continue
            start = half * height if isinstance(half, int) else pl.multiple_of(half * height, height)
            outs[out][f, pl.ds(start, height), dest] = source[rows, cols]

    yl = place[8]
    for s in range(4):
        for half in range(2):
            put(own[s].at[half], place[s], half)
        put(got[s], place[4 + s], yl)
        put(rest[s], place[4 + s], 1 - yl)


def assemble(pieces, plan, shapes, place):
    return build(
        functools.partial(assemble_kernel, plan),
        [(s, BF16) for s in shapes],
        place,
        *pieces["own"],
        *pieces["got"],
        *pieces["rest"],
        name="assemble",
    )


ALL = slice(0, D)
FIRST_PLAN = [
    (slice(0, 64), ALL, 0, 64, ALL),
    (slice(64, 80), slice(0, 128), 1, 16, slice(0, 128)),
    (slice(80, 144), ALL, 2, 64, ALL),
    (slice(144, 208), ALL, 2, 64, slice(D, 2 * D)),
    (slice(208, 272), ALL, 3, 0, ALL),
]
HEAD_PLAN = [
    (slice(0, 64), ALL, 0, 64, ALL),
    (slice(64, 128), slice(0, HALF), 0, 64, slice(D, D + HALF)),
    (slice(64, 128), slice(HALF, D), 1, 64, slice(0, HALF)),
]


def upper_kernel(pieces, w_in, w_out):
    for part in range(4):
        rows = pl.ds(part * 32, 32)
        w_in[:, rows, 0:D] = pieces[part, :, 0:32, :]
        w_in[:, rows, D : 2 * D] = pieces[part, :, 32:64, :]
        w_out[part] = pieces[part, :, 64:96, :]


def dot(left, right, dims=((1,), (0,))):
    return lax.dot_general(left, right, (dims, ((), ())), preferred_element_type=F32)


def dot_t(left, right):
    return dot(left, right, ((1,), (1,)))


def t_dot(left, right):
    return dot(left, right, ((0,), (0,)))


def normalize(stream, gain):
    scale = lax.rsqrt(jnp.mean(stream * stream, axis=-1, keepdims=True) + EPSILON)
    return (stream * scale * gain).astype(BF16), scale


def norm_back(stream, scale, gain, upstream):
    weighted = upstream * gain
    inner = jnp.mean(weighted * stream, axis=-1, keepdims=True)
    grad = scale * (weighted - stream * scale * scale * inner)
    return grad, jnp.sum(upstream * stream * scale, axis=0)


def add_cores(partial):
    return partial + swap_core(partial.astype(BF16)).astype(F32)


def lane_mask(shape, head):
    lane = lax.broadcasted_iota(jnp.int32, shape, 1)
    return (lane // 64) == head


def window_mask(block, first):
    i = lax.broadcasted_iota(jnp.int32, (128, 192), 0)
    j = lax.broadcasted_iota(jnp.int32, (128, 192), 1)
    allowed = (j > i) & (j <= i + REACH)
    if block == 0:
        allowed = allowed & ((j >= REACH) | (first == 0))
    return allowed


def probabilities(q, k, allowed):
    scores = jnp.where(allowed, dot_t(q, k) * SCALE, MASKED)
    weights = jnp.exp(scores - jnp.max(scores, axis=-1, keepdims=True))
    return weights / jnp.sum(weights, axis=-1, keepdims=True)


def attend_kernel(first_ref, q_ref, k_ref, v_ref, o_ref):
    for block in range(2):
        allowed = window_mask(block, first_ref[0])
        rows, keys = pl.ds(block * 128, 128), pl.ds(block * 128, 192)
        for pair in range(4):
            cols = pl.ds(pair * 128, 128)
            q, k, v = q_ref[rows, cols], k_ref[keys, cols], v_ref[keys, cols]
            outs = []
            for head in range(2):
                q_head = jnp.where(lane_mask(q.shape, head), q, jnp.zeros_like(q))
                p = probabilities(q_head, k, allowed)
                outs.append(dot(p.astype(BF16), v))
            o_ref[rows, cols] = jnp.where(lane_mask(q.shape, 0), outs[0], outs[1]).astype(BF16)


def attend(first, q, k_ext, v_ext):
    return pl.pallas_call(
        attend_kernel,
        out_shape=jax.ShapeDtypeStruct((PAIR, HALF), BF16),
        in_specs=[pl.BlockSpec(memory_space=pltpu.SMEM)]
        + [pl.BlockSpec(memory_space=pltpu.VMEM)] * 3,
        out_specs=pl.BlockSpec(memory_space=pltpu.VMEM),
        name="attend",
    )(first, q, k_ext, v_ext)


def attend_back_kernel(first_ref, q_ref, k_ref, v_ref, ep_ref, eq_ref, ek_ref, ev_ref):
    for pair in range(4):
        cols = pl.ds(pair * 128, 128)
        eks, evs = [], []
        for block in range(2):
            allowed = window_mask(block, first_ref[0])
            rows, keys = pl.ds(block * 128, 128), pl.ds(block * 128, 192)
            q, k, v = q_ref[rows, cols], k_ref[keys, cols], v_ref[keys, cols]
            ep = ep_ref[rows, cols]
            eq_out, ek_out, ev_out = [], [], []
            for head in range(2):
                own = lane_mask(q.shape, head)
                p = probabilities(jnp.where(own, q, jnp.zeros_like(q)), k, allowed)
                dp = dot_t(jnp.where(own, ep, jnp.zeros_like(ep)), v)
                inner = jnp.sum(p * dp, axis=-1, keepdims=True)
                es = (p * (dp - inner)).astype(BF16)
                ev_out.append(t_dot(p.astype(BF16), ep))
                ek_out.append(t_dot(es, q))
                eq_out.append(dot(es, k))
            pick_q = lane_mask((128, 128), 0)
            pick_k = lane_mask((192, 128), 0)
            eq_ref[rows, cols] = (jnp.where(pick_q, eq_out[0], eq_out[1]) * SCALE).astype(BF16)
            eks.append(jnp.where(pick_k, ek_out[0], ek_out[1]) * SCALE)
            evs.append(jnp.where(pick_k, ev_out[0], ev_out[1]))
        for parts, ref in ((eks, ek_ref), (evs, ev_ref)):
            ref[pl.ds(0, 128), cols] = parts[0][:128]
            ref[pl.ds(128, 64), cols] = parts[0][128:] + parts[1][:64]
            ref[pl.ds(192, 128), cols] = parts[1][64:]


def attend_back(first, q, k_ext, v_ext, ep):
    return pl.pallas_call(
        attend_back_kernel,
        out_shape=[
            jax.ShapeDtypeStruct((PAIR, HALF), BF16),
            jax.ShapeDtypeStruct((PAIR + REACH, HALF), F32),
            jax.ShapeDtypeStruct((PAIR + REACH, HALF), F32),
        ],
        in_specs=[pl.BlockSpec(memory_space=pltpu.SMEM)]
        + [pl.BlockSpec(memory_space=pltpu.VMEM)] * 4,
        out_specs=[pl.BlockSpec(memory_space=pltpu.VMEM)] * 3,
        name="attend_back",
    )(first, q, k_ext, v_ext, ep)


def own_rows(value):
    return lax.dynamic_slice_in_dim(value, at("c") * ROWS, ROWS, 0)


def share_grads(quarters):
    return [quarters[0]] + [along_x(quarters[by], by) for by in range(1, 4)]


def from_chips(*values):
    return lax.all_gather(jnp.concatenate(values, axis=0), "x", axis=0, tiled=False)


def quarter(place, by, width, offset=0):
    start = jnp.bitwise_and(place[1] + by, 3) * width + offset
    return pl.ds(pl.multiple_of(start, 128), width)


def feed_back_kernel(place, act, third, branch, w_in, w_out, partial, *quarters):
    for by in range(4):
        cols, up_cols = quarter(place, by, 256), quarter(place, by, 256, D)
        grad_hidden = dot_t(branch[...], w_out[cols, :])
        gate_act, up_act = act[:, cols], act[:, up_cols]
        sig = 1.0 / (1.0 + jnp.exp(-gate_act))
        grad_gate = (grad_hidden * up_act * sig * (1.0 + gate_act * (1.0 - sig))).astype(BF16)
        grad_up = (grad_hidden * gate_act * sig).astype(BF16)
        out = quarters[by]
        out[:, 0:256] = grad_gate
        out[:, 256:512] = grad_up
        out[:, 512:768] = third[:, cols]
        piece = dot_t(grad_gate, w_in[:, cols]) + dot_t(grad_up, w_in[:, up_cols])
        if by == 0:
            partial[...] = piece
        else:
            partial[...] += piece


def head_pack_kernel(place, eq, ek_ext, ev_ext, back, eo, eqkv, *quarters):
    cut = PAIR - REACH
    eqkv[:, 0:HALF] = eq[...]
    for i, ref in enumerate((ek_ext, ev_ext)):
        cols = pl.ds((i + 1) * HALF, HALF)
        eqkv[0:cut, cols] = ref[REACH:PAIR, :].astype(BF16)
        tail = ref[PAIR : PAIR + REACH, :] + back[:, pl.ds(i * HALF, HALF)].astype(F32)
        eqkv[cut:PAIR, cols] = tail.astype(BF16)
    for by in range(4):
        for i in range(3):
            quarters[by][:, pl.ds(i * 128, 128)] = eqkv[:, quarter(place, by, 128, i * HALF)]
        quarters[by][:, 384:640] = eo[:, quarter(place, by, 256)]


def mixer_pack_kernel(place, e1, conv, gate, after, taps, emix, *rest):
    quarters, ec = rest[:4], rest[4]
    ec[0:PAIR, :] = e1[...] * gate[...]
    ec[PAIR : PAIR + 8, :] = after[...]
    esig = taps[0:1, :] * ec[0:PAIR, :]
    for m in (1, 2):
        esig = esig + taps[m : m + 1, :] * ec[m : m + PAIR, :]
    emix[:, 0:HALF] = esig.astype(BF16)
    emix[:, HALF:D] = (e1[...] * conv[...]).astype(BF16)
    for by in range(4):
        for i in range(2):
            quarters[by][:, pl.ds(i * 128, 128)] = emix[:, quarter(place, by, 128, i * HALF)]


def fill_rows(place, out, mine, near, far):
    core = place[0]
    out[0:PAIR, :] = mine[...]
    for by in range(1, 4):
        chip = jnp.bitwise_and(place[1] - by, 3)
        for ref, c in ((near, core), (far, 1 - core)):
            rows = pl.ds(pl.multiple_of(by * PAIR + c * ROWS, ROWS), ROWS)
            out[rows, :] = ref[chip, 0:ROWS, :]


def weight_grad_kernel(kind, place, mine, near, far, *rest):
    rest = list(rest)
    if kind == "feed":
        branch = [rest.pop(0) for _ in range(3)]
    if kind in ("heads", "lower"):
        hidden = rest.pop(0)
    if kind == "lower":
        shared = rest.pop(0)
    grads = [rest.pop(0) for _ in range(4)]
    if kind == "mixer":
        extra = rest.pop(0)
    out, normed, e = rest[:3]
    fill_rows(place, normed, mine, near, far)
    for by in range(4):
        e[pl.ds(by * PAIR, PAIR), :] = grads[by][...]
    width = {"mixer": 256, "heads": 384, "feed": 512, "lower": 512}[kind]
    for i in range(4):
        got = t_dot(normed[:, pl.ds(i * 256, 256)], e[:, 0:width]).astype(BF16)
        for j in range(4):
            out[j % 2, 2 * i + j // 2, 0:64, 0:width] = got[j * 64 : j * 64 + 64]
    if kind == "feed":
        fill_rows(place, normed, *branch)
        for k in range(4):
            got = t_dot(e[:, width:], normed[:, pl.ds(k * 256, 256)]).astype(BF16)
            for f in range(8):
                for yl in range(2):
                    out[yl, f, pl.ds(16 * k, 16), width:] = got[f * 32 + yl * 16 : f * 32 + yl * 16 + 16]
    if kind == "lower":
        for i in range(4):
            cols = pl.ds(i * 256, 256)
            total = t_dot(hidden[:, cols], e[0:PAIR, width:])
            for by in range(1, 4):
                chip = jnp.bitwise_and(place[1] - by, 3)
                total = total + t_dot(shared[chip, :, cols], e[pl.ds(by * PAIR, PAIR), width:])
            total = total.astype(BF16)
            for f in range(8):
                out[i // 2, f, pl.ds(i % 2 * 32, 32), width:] = total[f * 32 : f * 32 + 32]
    if kind == "heads":
        for i in range(2):
            total = t_dot(hidden[:, pl.ds(i * 256, 256)], e[0:PAIR, width:])
            for by in range(1, 4):
                chip = jnp.bitwise_and(place[1] - by, 3)
                for side in range(2):
                    part = near[chip, ROWS : 2 * ROWS, pl.ds(side * HALF + i * 256, 256)]
                    total = total + t_dot(part, e[pl.ds(by * PAIR + side * ROWS, ROWS), width:])
            total = total.astype(BF16)
            for j in range(4):
                for side in range(2):
                    out[side, 4 * i + j, 0:64, width:] = total[
                        j * 64 : j * 64 + 64, side * 128 : side * 128 + 128
                    ]
    if kind == "mixer":
        for yl in range(2):
            out[yl, :, 64:80, :] = extra[...]


def weight_grads(kind, place, normed, grads, branch=(), hidden=None, shared=None, extra=None):
    width = {"mixer": 256, "heads": 512, "feed": 768, "lower": 768}[kind]
    rows = 80 if kind == "mixer" else 64
    arrays, specs = [], []
    for group in (normed, branch):
        if group:
            mine, near, near_at, far, far_at = group
            height = near.shape[1] if kind == "heads" else ROWS
            block = pl.BlockSpec((4, height, D), lambda i, n=near_at: (0, n, 0))
            other = pl.BlockSpec((4, ROWS, D), lambda i, n=far_at: (0, n, 0))
            arrays += [mine, near, far]
            specs += [VMEM, block, other]
    for value in (hidden, shared):
        if value is not None:
            arrays.append(value)
            whole = value is hidden
            specs.append(VMEM if whole else pl.BlockSpec((4, PAIR, D), lambda i: (0, 0, 0)))
    more = list(grads) + ([] if extra is None else [extra])
    return pl.pallas_call(
        functools.partial(weight_grad_kernel, kind),
        grid=(1,),
        out_shape=jax.ShapeDtypeStruct((2, 8, rows, width), BF16),
        in_specs=[SMEM] + specs + [VMEM] * len(more),
        out_specs=VMEM,
        scratch_shapes=[
            pltpu.VMEM((4 * PAIR, D), BF16),
            pltpu.VMEM((4 * PAIR, grads[0].shape[1]), BF16),
        ],
        compiler_params=BIG,
        name="weight_grads",
    )(place, *arrays, *more)


def reduce_rows(packed):
    return lax.all_to_all(packed.reshape((16,) + packed.shape[2:]), SUMS, 0, 0, tiled=True)


def summed(parts):
    return jnp.sum(parts.astype(F32), axis=0).astype(BF16)


def each_part():
    return [(yl, x, c) for yl in range(2) for x in range(4) for c in range(2)]


def feed_out_kernel(by_columns, done, gate, up, down):
    for yl in range(2):
        rows = pl.ds(yl * 64, 64)
        for c in range(2):
            for start, ref in ((0, gate), (256, up)):
                for g in range(2):
                    parts = [
                        done[yl * 8 + x * 2 + c, :, pl.ds(start + g * 128, 128)].astype(F32)
                        for x in range(4)
                    ]
                    for i in range(4):
                        out = None
                        for x in range(4):
                            piece = pltpu.roll(parts[x], (x - i) % 4 * 32, 1)
                            keep = in_lanes(piece.shape, x, 32)
                            out = piece if out is None else jnp.where(keep, piece, out)
                        ref[rows, pl.ds((4 * g + i) * 256 + c * 128, 128)] = out
    for i, (yl, x, c) in enumerate(each_part()):
        if by_columns:
            rows = pl.ds(c * 128 + yl * 64, 64)
            down[rows, pl.ds(x * 256, 256)] = done[i, :, 512:768].astype(F32)
            continue
        for k in range(4):
            down[pl.ds(c * 128 + x * 32 + yl * 16, 16), pl.ds(k * 256, 256)] = done[
                i, pl.ds(16 * k, 16), 512:768
            ].astype(F32)


def head_out_kernel(done, q, k, v, out):
    low = in_lanes((64, 128), 0, 64)
    for i, (yl, x, c) in enumerate(each_part()):
        cols = pl.ds(x * 256 + yl * 128, 128)
        out[pl.ds(c * 64, 64), cols] = done[i, :, 384:512].astype(F32)
        if c == 1:
            continue
        rows = pl.ds(yl * 64, 64)
        for n, ref in enumerate((q, k, v)):
            lanes = pl.ds(n * 128, 128)
            a, b = done[i, :, lanes].astype(F32), done[i + 1, :, lanes].astype(F32)
            ref[rows, pl.ds(x * 256, 128)] = jnp.where(low, a, pltpu.roll(b, 64, 1))
            ref[rows, pl.ds(x * 256 + 128, 128)] = jnp.where(low, pltpu.roll(a, 64, 1), b)


def mixer_out_kernel(done, first, second, small):
    total = None
    for i, (yl, x, c) in enumerate(each_part()):
        rows, cols = pl.ds(yl * 64, 64), pl.ds(c * HALF + x * 128, 128)
        first[rows, cols] = done[i, 0:64, 0:128].astype(F32)
        second[rows, cols] = done[i, 0:64, 128:256].astype(F32)
        if yl == 0:
            piece = done[i, 64:80, 0:128].astype(F32)
            total = piece if total is None else total + piece
    small[...] = total


def finish(kernel, done, shapes):
    return pl.pallas_call(
        kernel,
        out_shape=[jax.ShapeDtypeStruct(s, F32) for s in shapes],
        in_specs=[VMEM],
        out_specs=[VMEM] * len(shapes),
        compiler_params=BIG,
        name="finish",
    )(done)


def body(
    inputs,
    cotangent,
    lengths,
    mixer_gain,
    mixer_input,
    mixer_gate,
    mixer_kernel,
    lower_gain,
    lower_gate,
    lower_up,
    lower_down,
    attention_gain,
    attention_query,
    attention_key,
    attention_value,
    attention_output,
    upper_gain,
    upper_gate,
    upper_up,
    upper_down,
):
    c, x, yl, yh, z = at("c"), at("x"), at("yl"), at("yh"), at("z")
    chip = yl * 4 + x
    first_chip = (chip == 0).astype(jnp.int32).reshape(1)
    zs = [jnp.mod(z - (1 - 2 * c) * s, 4) for s in range(4)]
    place = jnp.stack([yh * 4 + v for v in zs] + [(1 - yh) * 4 + v for v in zs] + [yl]).astype(
        jnp.int32
    )
    where = jnp.stack([c, x]).astype(jnp.int32)

    small = jnp.concatenate(
        [
            mixer_gain[None],
            lower_gain[None],
            attention_gain[None],
            upper_gain[None],
            mixer_kernel,
            jnp.zeros((9, ROWS), BF16),
        ],
        axis=0,
    )
    upper_part = build(
        upper_part_kernel,
        ((8, 96, D), BF16),
        where,
        upper_gate,
        upper_up,
        upper_down,
        name="upper_part",
    )
    upper_part = lax.all_to_all(upper_part, ("yh", "z"), 0, 0, tiled=True)
    first_slab = build(
        first_slab_kernel,
        ((2, 272, D), BF16),
        where,
        mixer_input,
        mixer_gate,
        small,
        lower_gate,
        lower_up,
        lower_down,
        name="first_slab",
    )
    head_slab = build(
        head_slab_kernel,
        ((2, 128, D), BF16),
        where,
        attention_query,
        attention_key,
        attention_value,
        attention_output,
        name="head_slab",
    )
    pieces, upper_part = gather_slabs([first_slab, head_slab], upper_part)
    upper_pieces = lax.all_gather(upper_part, "x", axis=0, tiled=False)

    mine = jnp.concatenate([inputs[0], cotangent[0]], axis=1)
    two = both_cores(mine, swap_core(mine))
    start = two[:, :D].astype(F32)
    place_row = chip * PAIR + jnp.arange(PAIR, dtype=jnp.int32)
    valid = (place_row < lengths[0]).astype(F32)
    e4 = two[:, D:].astype(F32) * valid[:, None]
    halo = chip_shift(two[PAIR - 16 :, :D], 1)

    mix_w, small_all, lower_in, lower_out = assemble(
        pieces[0],
        FIRST_PLAN,
        [(8, 128, D), (8, 32, 128), (8, 128, 2 * D), (4, 8, 32, D)],
        place,
    )
    mix_w = mix_w.reshape(D, D)
    lower_w = (lower_in.reshape(D, 2 * D), lower_out.reshape(D, D))
    small_all = small_all[:, :16].transpose(1, 0, 2).reshape(16, D).astype(F32)
    gain_m, gain_l, gain_a, gain_u = (small_all[i] for i in range(4))
    taps = lax.dynamic_slice_in_dim(small_all[4:7], c * HALF, HALF, 1)

    with_halo = jnp.concatenate([halo.astype(F32), start], axis=0)
    na_ext, _ = normalize(with_halo, gain_m)
    na = na_ext[16:]
    scale_a = lax.rsqrt(jnp.mean(start * start, axis=-1, keepdims=True) + EPSILON)
    both = dot(na_ext, mix_w)
    signal = both[:, :HALF].astype(BF16).astype(F32)
    gate = both[16:, HALF:]
    shifted = [signal[16:], signal[15:-1], signal[14:-2]]
    conv = sum(taps[m] * shifted[m] for m in range(3))
    mixed = conv * gate
    h1 = start + both_cores(mixed, swap_core(mixed.astype(BF16)).astype(F32), axis=1)

    def feed(stream, gain, weights):
        w_in, w_out = weights
        normed, scale = normalize(stream, gain)
        act = dot(normed, w_in)
        hidden = (jax.nn.silu(act[:, :D]) * act[:, D:]).astype(BF16)
        return normed, scale, act, hidden, dot(hidden, w_out)

    nb, scale_b, act_l, ha, part = feed(h1, gain_l, lower_w)
    h2 = h1 + add_cores(part)
    branch_u = e4.astype(BF16)
    near_1 = from_chips(ha, own_rows(branch_u), own_rows(nb), own_rows(na))

    qkv_w, out_w = assemble(pieces[1], HEAD_PLAN, [(8, 128, 3 * HALF), (8, 128, HALF)], place)
    qkv_w = qkv_w.reshape(D, 3 * HALF)
    out_w = out_w.reshape(8, 2, 64, HALF).transpose(0, 2, 1, 3).reshape(HALF, D)
    nc, scale_c = normalize(h2, gain_a)
    qkv = dot(nc, qkv_w).astype(BF16)
    q = qkv[:, :HALF]
    edge = chip_shift(qkv[PAIR - REACH :, HALF:], 1)
    kv_ext = jnp.concatenate([edge, qkv[:, HALF:]], axis=0)
    k_ext, v_ext = kv_ext[:, :HALF], kv_ext[:, HALF:]
    o = attend(first_chip, q, k_ext, v_ext)
    h3 = h2 + add_cores(dot(o, out_w))

    upper_in, upper_out = pl.pallas_call(
        upper_kernel,
        out_shape=[
            jax.ShapeDtypeStruct((8, 128, 2 * D), BF16),
            jax.ShapeDtypeStruct((4, 8, 32, D), BF16),
        ],
        in_specs=[VMEM],
        out_specs=[VMEM] * 2,
        compiler_params=BIG,
        name="upper_weights",
    )(upper_pieces)
    upper_w = (upper_in.reshape(D, 2 * D), upper_out.reshape(D, D))
    nd, scale_d, act_u, hb, part = feed(h3, gain_u, upper_w)
    near_u = from_chips(own_rows(nd))
    other_part = lax.dynamic_slice_in_dim(part, (1 - c) * ROWS, ROWS, 0).astype(BF16)
    outputs = own_rows(h3) + own_rows(part) + swap_core(other_part).astype(F32)

    def feed_back(weights, act, hidden, branch):
        out = build(
            feed_back_kernel,
            [((PAIR, D), F32)] + [((PAIR, 768), BF16)] * 4,
            where,
            act,
            branch if hidden is None else hidden,
            branch,
            *weights,
            name="feed_back",
        )
        return out[0], share_grads(out[1:])

    partial, grads_u = feed_back(upper_w, act_u, hb, branch_u)
    o_rows = jnp.concatenate([o[:ROWS], o[ROWS:]], axis=1)
    grad_stream, gain_grad_u = norm_back(h3, scale_d, gain_u, add_cores(partial))
    e3 = e4 + grad_stream
    eo = e3.astype(BF16)
    ep = dot_t(eo, out_w).astype(BF16)
    eq, ek_ext, ev_ext = attend_back(first_chip, q, k_ext, v_ext, ep)
    eq, ek_ext, ev_ext, near_1, nc, *grads_u = tie([eq, ek_ext, ev_ext, near_1, nc, *grads_u], [])
    near_2 = from_chips(own_rows(nc), o_rows)
    ekv_edge = jnp.concatenate([ek_ext[:REACH], ev_ext[:REACH]], axis=1).astype(BF16)
    back = chip_shift(ekv_edge, -1)
    eqkv, *quarters = build(
        head_pack_kernel,
        [((PAIR, 3 * HALF), BF16)] + [((PAIR, 640), BF16)] * 4,
        where,
        eq,
        ek_ext,
        ev_ext,
        back,
        eo,
        name="head_pack",
    )
    eqkv, near_u, *quarters = tie([eqkv, near_u, *quarters], [])

    grads_a = share_grads(quarters)
    far_u = swap_core(near_u)
    far_1 = swap_core(near_1[:, PAIR:])
    packed = weight_grads(
        "feed", where, (nd, near_u, 0, far_u, 0), grads_u, (branch_u, near_1, 2, far_1, 0)
    )
    eqkv, packed = tie([eqkv, packed], [])
    sum_u = reduce_rows(packed)
    grad_nc = add_cores(dot_t(eqkv, qkv_w))
    grad_stream, gain_grad_a = norm_back(h2, scale_c, gain_a, grad_nc)
    e2 = e3 + grad_stream
    partial, grads_l = feed_back(lower_w, act_l, None, e2.astype(BF16))
    partial, sum_u, near_2, *grads_a = tie([partial, sum_u, near_2, *grads_a], [])

    packed = weight_grads(
        "heads", where, (nc, near_2, 0, swap_core(near_2[:, :ROWS]), 0), grads_a, hidden=o
    )
    partial, packed = tie([partial, packed], [])
    sum_a = reduce_rows(packed)
    done_u = lax.all_gather(summed(sum_u), SEQ, axis=0, tiled=False)
    grad_stream, gain_grad_l = norm_back(h1, scale_b, gain_l, add_cores(partial))
    e1 = e2 + grad_stream
    e1_own = lax.dynamic_slice_in_dim(e1, c * HALF, HALF, 1)
    ec = e1_own * gate
    tap_grads = jnp.stack([jnp.sum(ec * shifted[m], axis=0) for m in range(3)])
    ec_next = chip_shift(ec[:8], -1)
    emix, *quarters = pl.pallas_call(
        mixer_pack_kernel,
        out_shape=[jax.ShapeDtypeStruct((PAIR, D), BF16)]
        + [jax.ShapeDtypeStruct((PAIR, 256), BF16)] * 4,
        in_specs=[SMEM] + [VMEM] * 5,
        out_specs=[VMEM] * 5,
        scratch_shapes=[pltpu.VMEM((PAIR + 8, HALF), F32)],
        compiler_params=BIG,
        name="mixer_pack",
    )(where, e1_own, conv, gate, ec_next, jnp.pad(taps, ((0, 5), (0, 0))))
    emix, sum_a, *moved = tie([emix, sum_a, *quarters, *grads_l], [])
    quarters, grads_l = moved[:4], moved[4:]

    grads_m = share_grads(quarters)
    packed = weight_grads(
        "lower", where, (nb, near_1, 3, far_1, 1), grads_l, hidden=ha, shared=near_1
    )
    emix, packed = tie([emix, packed], [])
    sum_l = reduce_rows(packed)
    done_a = lax.all_gather(summed(sum_a), SEQ, axis=0, tiled=False)
    grad_na = dot_t(emix, mix_w)
    other_na = lax.dynamic_slice_in_dim(grad_na, (1 - c) * ROWS, ROWS, 0).astype(BF16)
    grad_na = own_rows(grad_na) + swap_core(other_na).astype(F32)
    grad_start, gain_grad_m = norm_back(own_rows(start), own_rows(scale_a), gain_m, grad_na)
    input_grad = own_rows(e1) + grad_start
    once = (c == 0).astype(F32)
    wide_taps = lax.dynamic_update_slice(jnp.zeros((3, D), F32), tap_grads, (0, c * HALF))
    gains = jnp.stack([gain_grad_m, gain_grad_l * once, gain_grad_a * once, gain_grad_u * once])
    extra = jnp.concatenate([gains, wide_taps], axis=0).reshape(7, 8, ROWS).transpose(1, 0, 2)
    extra = jnp.pad(extra.astype(BF16), ((0, 0), (0, 9), (0, ROWS)))
    extra, sum_l, *grads_m = tie([extra, sum_l, *grads_m], [])

    packed = weight_grads(
        "mixer", where, (na, near_1, 4, far_1, 2), grads_m, extra=extra
    )
    (sum_l, packed) = tie([sum_l, packed], [])
    sum_m = reduce_rows(packed)
    done_l = lax.all_gather(summed(sum_l), SEQ, axis=0, tiled=False)
    done_m = spread(summed(sum_m), SEQ, 16)
    feed_shapes = [(ROWS, 2 * D), (ROWS, 2 * D), (2 * ROWS, D)]
    upper_grads = finish(functools.partial(feed_out_kernel, False), done_u, feed_shapes)
    head_grads = finish(head_out_kernel, done_a, [(ROWS, D)] * 4)
    lower_grads = finish(functools.partial(feed_out_kernel, True), done_l, feed_shapes)
    in_grad, gate_grad, tail = finish(
        mixer_out_kernel, done_m, [(ROWS, D), (ROWS, D), (16, ROWS)]
    )
    return (
        outputs.astype(BF16)[None],
        input_grad[None],
        tail[0],
        in_grad,
        gate_grad,
        tail[4:7],
        tail[1],
        *lower_grads,
        tail[2],
        *head_grads,
        tail[3],
        *upper_grads,
    )


def solution(mesh):
    fine = Mesh(mesh.devices.reshape(SIZES), AXES)
    rows = ("yh", "z")
    slots = P(rows, SEQ, None)
    vector, matrix, columns = P(rows), P(rows, None), P(None, rows)
    weights = (
        (vector, matrix, matrix, columns)
        + (vector, matrix, matrix, matrix)
        + (vector, matrix, matrix, matrix, matrix)
        + (vector, matrix, matrix, matrix)
    )
    return jax.shard_map(
        body,
        mesh=fine,
        in_specs=(slots, slots, vector) + weights,
        out_specs=(slots, slots) + weights,
        check_vma=False,
    )
```

```python
import functools

import jax
import jax.numpy as jnp
from jax import lax
from jax.experimental import pallas as pl
from jax.experimental.pallas import tpu as pltpu
from jax.sharding import Mesh
from jax.sharding import PartitionSpec as P

EPSILON = 1e-05
MASKED = -1e30
AXES = ("yl", "x", "c", "yh", "z")
SIZES = (2, 4, 2, 2, 4)
SEQ = ("yl", "x", "c")
SUMS = ("yl", "yh", "z")
F32 = jnp.float32
BF16 = jnp.bfloat16
ROWS = 128
PAIR = 256
D = 1024
HALF = 512
REACH = 64
SCALE = 64 ** (-0.5)


def at(axis):
    return lax.axis_index(axis)


def swap_core(value):
    return lax.ppermute(value, "c", [(0, 1), (1, 0)])


def hop_z(value):
    pairs = [(c * 4 + z, c * 4 + (z + 1 - 2 * c) % 4) for c in range(2) for z in range(4)]
    return lax.ppermute(value, ("c", "z"), pairs)


def cross(value):
    return lax.ppermute(value, ("yl", "yh"), [(0, 3), (3, 0), (1, 2), (2, 1)])


def swap_yl(value):
    return lax.ppermute(value, "yl", [(0, 1), (1, 0)])


def chip_shift(value, by):
    pairs = [(i, i + by) for i in range(8) if 0 <= i + by < 8]
    return lax.ppermute(value, ("yl", "x"), pairs)


def along_x(value, by):
    return lax.ppermute(value, "x", [(i, (i + by) % 4) for i in range(4)])


def spread(value, axes, count):
    return lax.all_to_all(
        jnp.broadcast_to(value[None], (count,) + value.shape), axes, 0, 0, tiled=True
    )


def tie(values, after):
    out = lax.optimization_barrier(tuple(values) + tuple(after))
    return out[: len(values)]


def both_cores(own, other, axis=0):
    first = at("c") == 0
    return jnp.concatenate(
        [jnp.where(first, own, other), jnp.where(first, other, own)], axis=axis
    )


VMEM = pl.BlockSpec(memory_space=pltpu.VMEM)
SMEM = pl.BlockSpec(memory_space=pltpu.SMEM)
BIG = pltpu.CompilerParams(vmem_limit_bytes=40 * 1024 * 1024)


def in_lanes(shape, which, width):
    return lax.broadcasted_iota(jnp.int32, shape, 1) // width == which


def hidden_blocks(ref, rows, core):
    blocks = [
        ref[rows, pl.ds(pl.multiple_of(f * 256 + core * 128, 128), 128)].astype(F32)
        for f in range(8)
    ]
    for b in range(8):
        out = None
        for i in range(4):
            source = blocks[4 * (b % 2) + i]
            piece = pltpu.roll(source, (i - b // 2) % 4 * 32, 1)
            out = piece if out is None else jnp.where(in_lanes(piece.shape, i, 32), piece, out)
        yield b, out.astype(BF16)


def head_block(ref, rows, block, core):
    left = ref[rows, pl.ds(block * 256, 128)].astype(F32)
    right = ref[rows, pl.ds(block * 256 + 128, 128)].astype(F32)
    low = lax.broadcasted_iota(jnp.int32, left.shape, 1) < 64
    first = jnp.where(low, left, pltpu.roll(right, 64, 1))
    second = jnp.where(low, pltpu.roll(left, 64, 1), right)
    return jnp.where(core == 0, first, second).astype(BF16)


def first_slab_kernel(place, m_in, m_gate, small, gate, up, down, out):
    core = place[0]
    for half in range(2):
        rows = pl.ds(half * 64, 64)
        for i, ref in enumerate((m_in, m_gate)):
            out[half, 0:64, pl.ds(i * HALF, HALF)] = ref[
                rows, pl.ds(pl.multiple_of(core * HALF, HALF), HALF)
            ]
        out[half, 64:80, :] = jnp.zeros((16, D), BF16)
        out[half, 64:80, 0:128] = small[...]
        for start, ref in ((80, gate), (144, up)):
            for block, value in hidden_blocks(ref, rows, core):
                out[half, pl.ds(start, 64), pl.ds(block * 128, 128)] = value
        out[half, 208:272, :] = down[pl.ds(pl.multiple_of(core * 128 + half * 64, 64), 64), :]


def head_slab_kernel(place, q, k, v, wo, out):
    core = place[0]
    for half in range(2):
        rows = pl.ds(half * 64, 64)
        for block in range(4):
            out[half, 0:64, pl.ds(block * 128, 128)] = head_block(q, rows, block, core)
            out[half, 0:64, pl.ds(512 + block * 128, 128)] = head_block(k, rows, block, core)
            out[half, 64:128, pl.ds(block * 128, 128)] = head_block(v, rows, block, core)
        out[half, 64:128, 512:1024] = wo[
            pl.ds(pl.multiple_of(core * 64, 64), 64), pl.ds(half * HALF, HALF)
        ]


def upper_part_kernel(place, gate, up, down, out):
    core, part = place[0], place[1]
    rows = pl.ds(pl.multiple_of(part * 32, 32), 32)
    low = down[pl.ds(pl.multiple_of(core * 128 + part * 32, 32), 32), :]
    for copy in range(8):
        out[copy, 64:96, :] = low
    for start, ref in ((0, gate), (32, up)):
        for block, value in hidden_blocks(ref, rows, core):
            for copy in range(8):
                out[copy, pl.ds(start, 32), pl.ds(block * 128, 128)] = value


def build(kernel, shapes, place, *arrays, name):
    many = isinstance(shapes, list)
    return pl.pallas_call(
        kernel,
        out_shape=[jax.ShapeDtypeStruct(*s) for s in shapes]
        if many
        else jax.ShapeDtypeStruct(*shapes),
        in_specs=[SMEM] + [VMEM] * len(arrays),
        out_specs=[VMEM] * len(shapes) if many else VMEM,
        compiler_params=BIG,
        name=name,
    )(place, *arrays)


def gather_slabs(slabs, other):
    yl = at("yl")
    state = [dict(own=[s], got=[], rest=[]) for s in slabs]
    moved = []
    for step in range(4 * len(slabs) + 1):
        if moved:
            values = [st[key][-1] for st, key in moved]
            if step == 1:
                *values, other = tie([*values, other], [])
            else:
                values = tie(values, [])
            for (st, key), value in zip(moved, values):
                st[key][-1] = value
        moved, made = [], []
        for g, st in enumerate(state):
            k = step - 4 * g
            if 0 <= k < 3:
                made.append((st, "own", hop_z(st["own"][k])))
            if 1 <= k < 5:
                made.append((st, "rest", swap_yl(st["got"][k - 1])))
            if 0 <= k < 4:
                half = lax.dynamic_index_in_dim(st["own"][k], 1 - yl, 0, keepdims=False)
                made.append((st, "got", cross(half)))
        for st, key, value in made:
            st[key].append(value)
            moved.append((st, key))
    return state, other


def assemble_kernel(plan, place, *refs):
    own, got, rest = refs[0:4], refs[4:8], refs[8:12]
    outs = refs[12:]

    def put(source, f, half):
        for rows, cols, out, height, dest in plan:
            if height == 0:
                for i in range(2):
                    outs[out][half * 2 + i, f] = source[rows.start + i * 32 : rows.start + i * 32 + 32]
                continue
            size = height or HALF
            start = half * size if isinstance(half, int) else pl.multiple_of(half * size, size)
            if height is None:
                outs[out][f, :, pl.ds(start, size)] = source[rows, cols]
            else:
                outs[out][f, pl.ds(start, size), dest] = source[rows, cols]

    yl = place[8]
    for s in range(4):
        for half in range(2):
            put(own[s].at[half], place[s], half)
        put(got[s], place[4 + s], yl)
        put(rest[s], place[4 + s], 1 - yl)


def assemble(pieces, plan, shapes, place):
    return build(
        functools.partial(assemble_kernel, plan),
        [(s, BF16) for s in shapes],
        place,
        *pieces["own"],
        *pieces["got"],
        *pieces["rest"],
        name="assemble",
    )


ALL = slice(0, D)
FIRST_PLAN = [
    (slice(0, 64), ALL, 0, 64, ALL),
    (slice(64, 80), slice(0, 128), 1, 16, slice(0, 128)),
    (slice(80, 144), ALL, 2, 64, ALL),
    (slice(144, 208), ALL, 2, 64, slice(D, 2 * D)),
    (slice(208, 272), ALL, 3, 0, ALL),
]
HEAD_PLAN = [
    (slice(0, 64), ALL, 0, 64, ALL),
    (slice(64, 128), slice(0, HALF), 0, 64, slice(D, D + HALF)),
    (slice(64, 128), slice(HALF, D), 1, None, None),
]


def upper_kernel(pieces, w_in, w_out):
    for part in range(4):
        rows = pl.ds(part * 32, 32)
        w_in[:, rows, 0:D] = pieces[part, :, 0:32, :]
        w_in[:, rows, D : 2 * D] = pieces[part, :, 32:64, :]
        w_out[part] = pieces[part, :, 64:96, :]


def dot(left, right, dims=((1,), (0,))):
    return lax.dot_general(left, right, (dims, ((), ())), preferred_element_type=F32)


def dot_t(left, right):
    return dot(left, right, ((1,), (1,)))


def t_dot(left, right):
    return dot(left, right, ((0,), (0,)))


def normalize(stream, gain):
    scale = lax.rsqrt(jnp.mean(stream * stream, axis=-1, keepdims=True) + EPSILON)
    return (stream * scale * gain).astype(BF16), scale


def norm_back(stream, scale, gain, upstream):
    weighted = upstream * gain
    inner = jnp.mean(weighted * stream, axis=-1, keepdims=True)
    grad = scale * (weighted - stream * scale * scale * inner)
    return grad, jnp.sum(upstream * stream * scale, axis=0)


def add_cores(partial):
    return partial + swap_core(partial.astype(BF16)).astype(F32)


def lane_mask(shape, head):
    lane = lax.broadcasted_iota(jnp.int32, shape, 1)
    return (lane // 64) == head


def window_mask(block, first):
    i = lax.broadcasted_iota(jnp.int32, (128, 192), 0)
    j = lax.broadcasted_iota(jnp.int32, (128, 192), 1)
    allowed = (j > i) & (j <= i + REACH)
    if block == 0:
        allowed = allowed & ((j >= REACH) | (first == 0))
    return allowed


def probabilities(q, k, allowed):
    scores = jnp.where(allowed, dot_t(q, k) * SCALE, MASKED)
    weights = jnp.exp(scores - jnp.max(scores, axis=-1, keepdims=True))
    return weights / jnp.sum(weights, axis=-1, keepdims=True)


def attend_kernel(first_ref, q_ref, k_ref, v_ref, o_ref):
    for block in range(2):
        allowed = window_mask(block, first_ref[0])
        rows, keys = pl.ds(block * 128, 128), pl.ds(block * 128, 192)
        for pair in range(4):
            cols = pl.ds(pair * 128, 128)
            q, k, v = q_ref[rows, cols], k_ref[keys, cols], v_ref[keys, cols]
            outs = []
            for head in range(2):
                q_head = jnp.where(lane_mask(q.shape, head), q, jnp.zeros_like(q))
                p = probabilities(q_head, k, allowed)
                outs.append(dot(p.astype(BF16), v))
            o_ref[rows, cols] = jnp.where(lane_mask(q.shape, 0), outs[0], outs[1]).astype(BF16)


def attend(first, q, k_ext, v_ext):
    return pl.pallas_call(
        attend_kernel,
        out_shape=jax.ShapeDtypeStruct((PAIR, HALF), BF16),
        in_specs=[pl.BlockSpec(memory_space=pltpu.SMEM)]
        + [pl.BlockSpec(memory_space=pltpu.VMEM)] * 3,
        out_specs=pl.BlockSpec(memory_space=pltpu.VMEM),
        name="attend",
    )(first, q, k_ext, v_ext)


def attend_back_kernel(first_ref, q_ref, k_ref, v_ref, ep_ref, eq_ref, ek_ref, ev_ref):
    for pair in range(4):
        cols = pl.ds(pair * 128, 128)
        eks, evs = [], []
        for block in range(2):
            allowed = window_mask(block, first_ref[0])
            rows, keys = pl.ds(block * 128, 128), pl.ds(block * 128, 192)
            q, k, v = q_ref[rows, cols], k_ref[keys, cols], v_ref[keys, cols]
            ep = ep_ref[rows, cols]
            eq_out, ek_out, ev_out = [], [], []
            for head in range(2):
                own = lane_mask(q.shape, head)
                p = probabilities(jnp.where(own, q, jnp.zeros_like(q)), k, allowed)
                dp = dot_t(jnp.where(own, ep, jnp.zeros_like(ep)), v)
                inner = jnp.sum(p * dp, axis=-1, keepdims=True)
                es = (p * (dp - inner)).astype(BF16)
                ev_out.append(t_dot(p.astype(BF16), ep))
                ek_out.append(t_dot(es, q))
                eq_out.append(dot(es, k))
            pick_q = lane_mask((128, 128), 0)
            pick_k = lane_mask((192, 128), 0)
            eq_ref[rows, cols] = (jnp.where(pick_q, eq_out[0], eq_out[1]) * SCALE).astype(BF16)
            eks.append(jnp.where(pick_k, ek_out[0], ek_out[1]) * SCALE)
            evs.append(jnp.where(pick_k, ev_out[0], ev_out[1]))
        for parts, ref in ((eks, ek_ref), (evs, ev_ref)):
            ref[pl.ds(0, 128), cols] = parts[0][:128]
            ref[pl.ds(128, 64), cols] = parts[0][128:] + parts[1][:64]
            ref[pl.ds(192, 128), cols] = parts[1][64:]


def attend_back(first, q, k_ext, v_ext, ep):
    return pl.pallas_call(
        attend_back_kernel,
        out_shape=[
            jax.ShapeDtypeStruct((PAIR, HALF), BF16),
            jax.ShapeDtypeStruct((PAIR + REACH, HALF), F32),
            jax.ShapeDtypeStruct((PAIR + REACH, HALF), F32),
        ],
        in_specs=[pl.BlockSpec(memory_space=pltpu.SMEM)]
        + [pl.BlockSpec(memory_space=pltpu.VMEM)] * 4,
        out_specs=[pl.BlockSpec(memory_space=pltpu.VMEM)] * 3,
        name="attend_back",
    )(first, q, k_ext, v_ext, ep)


def own_rows(value):
    return lax.dynamic_slice_in_dim(value, at("c") * ROWS, ROWS, 0)


def share_grads(quarters):
    return [quarters[0]] + [along_x(quarters[by], by) for by in range(1, 4)]


def from_chips(*values):
    return lax.all_gather(jnp.concatenate(values, axis=0), "x", axis=0, tiled=False)


def quarter(place, by, width, offset=0):
    start = jnp.bitwise_and(place[1] + by, 3) * width + offset
    return pl.ds(pl.multiple_of(start, 128), width)


def carry_rows(place, out, first, normed):
    rows = pl.ds(pl.multiple_of(place[0] * ROWS, ROWS), ROWS)
    for side in range(2):
        part = normed[rows, pl.ds(side * HALF, HALF)]
        out[pl.ds(side * ROWS, ROWS), pl.ds(first, HALF)] = part


def feed_back_kernel(upper, place, act, third, normed, branch, w_in, w_out, partial, *quarters):
    for by in range(4):
        cols, up_cols = quarter(place, by, 256), quarter(place, by, 256, D)
        grad_hidden = dot_t(branch[...], w_out[cols, :])
        gate_act, up_act = act[:, cols], act[:, up_cols]
        sig = 1.0 / (1.0 + jnp.exp(-gate_act))
        grad_gate = (grad_hidden * up_act * sig * (1.0 + gate_act * (1.0 - sig))).astype(BF16)
        grad_up = (grad_hidden * gate_act * sig).astype(BF16)
        out = quarters[by]
        out[:, 0:256] = grad_gate
        out[:, 256:512] = grad_up
        out[:, 512:768] = third[:, cols]
        if upper:
            carry_rows(place, out, 768, normed)
        piece = dot_t(grad_gate, w_in[:, cols]) + dot_t(grad_up, w_in[:, up_cols])
        if by == 0:
            partial[...] = piece
        else:
            partial[...] += piece


def head_pack_kernel(place, eq, ek_ext, ev_ext, back, eo, eqkv, *quarters):
    cut = PAIR - REACH
    eqkv[:, 0:HALF] = eq[...]
    for i, ref in enumerate((ek_ext, ev_ext)):
        cols = pl.ds((i + 1) * HALF, HALF)
        eqkv[0:cut, cols] = ref[REACH:PAIR, :].astype(BF16)
        tail = ref[PAIR : PAIR + REACH, :] + back[:, pl.ds(i * HALF, HALF)].astype(F32)
        eqkv[cut:PAIR, cols] = tail.astype(BF16)
    for by in range(4):
        for i in range(3):
            quarters[by][:, pl.ds(i * 128, 128)] = eqkv[:, quarter(place, by, 128, i * HALF)]
        quarters[by][:, 384:640] = eo[:, quarter(place, by, 256)]


def mixer_pack_kernel(place, e1, conv, gate, after, taps, emix, *rest):
    quarters, ec = rest[:4], rest[4]
    ec[0:PAIR, :] = e1[...] * gate[...]
    ec[PAIR : PAIR + 8, :] = after[...]
    esig = taps[0:1, :] * ec[0:PAIR, :]
    for m in (1, 2):
        esig = esig + taps[m : m + 1, :] * ec[m : m + PAIR, :]
    emix[:, 0:HALF] = esig.astype(BF16)
    emix[:, HALF:D] = (e1[...] * conv[...]).astype(BF16)
    for by in range(4):
        for i in range(2):
            quarters[by][:, pl.ds(i * 128, 128)] = emix[:, quarter(place, by, 128, i * HALF)]


def fill_rows(place, out, mine, near, far):
    core = place[0]
    out[0:PAIR, :] = mine[...]
    for by in range(1, 4):
        chip = jnp.bitwise_and(place[1] - by, 3)
        for ref, c in ((near, core), (far, 1 - core)):
            rows = pl.ds(pl.multiple_of(by * PAIR + c * ROWS, ROWS), ROWS)
            out[rows, :] = ref[chip, 0:ROWS, :]


def fill_carried(place, out, mine, far, grads, first):
    core = place[0]
    out[0:PAIR, :] = mine[...]
    for by in range(1, 4):
        near_rows = pl.ds(pl.multiple_of(by * PAIR + core * ROWS, ROWS), ROWS)
        far_rows = pl.ds(pl.multiple_of(by * PAIR + (1 - core) * ROWS, ROWS), ROWS)
        for side in range(2):
            rows, cols = pl.ds(side * ROWS, ROWS), pl.ds(side * HALF, HALF)
            out[near_rows, cols] = grads[by][rows, pl.ds(first, HALF)]
            out[far_rows, cols] = far[by - 1, rows, :]


def weight_grad_kernel(kind, place, mine, *rest):
    rest = list(rest)
    near = rest.pop(0) if kind != "feed" else None
    far = rest.pop(0)
    if kind == "feed":
        branch = [rest.pop(0) for _ in range(3)]
    if kind in ("heads", "lower"):
        hidden = rest.pop(0)
    if kind == "lower":
        shared = rest.pop(0)
    grads = [rest.pop(0) for _ in range(4)]
    if kind == "mixer":
        extra = rest.pop(0)
    out, normed, e = rest[:3]
    every = e.shape[1]
    if near is None:
        fill_carried(place, normed, mine, far, grads, every)
    else:
        fill_rows(place, normed, mine, near, far)
    for by in range(4):
        e[pl.ds(by * PAIR, PAIR), :] = grads[by][:, 0:every]
    width = {"mixer": 256, "heads": 384, "feed": 512, "lower": 512}[kind]
    for i in range(4):
        got = t_dot(normed[:, pl.ds(i * 256, 256)], e[:, 0:width]).astype(BF16)
        for j in range(4):
            out[j % 2, 2 * i + j // 2, 0:64, 0:width] = got[j * 64 : j * 64 + 64]
    if kind == "feed":
        fill_rows(place, normed, *branch)
        for k in range(4):
            got = t_dot(e[:, width:], normed[:, pl.ds(k * 256, 256)]).astype(BF16)
            for f in range(8):
                for yl in range(2):
                    out[yl, f, pl.ds(16 * k, 16), width:] = got[f * 32 + yl * 16 : f * 32 + yl * 16 + 16]
    if kind == "lower":
        for i in range(4):
            cols = pl.ds(i * 256, 256)
            total = t_dot(hidden[:, cols], e[0:PAIR, width:])
            for by in range(1, 4):
                chip = jnp.bitwise_and(place[1] - by, 3)
                total = total + t_dot(shared[chip, :, cols], e[pl.ds(by * PAIR, PAIR), width:])
            total = total.astype(BF16)
            for f in range(8):
                out[i // 2, f, pl.ds(i % 2 * 32, 32), width:] = total[f * 32 : f * 32 + 32]
    if kind == "heads":
        for i in range(2):
            total = t_dot(hidden[:, pl.ds(i * 256, 256)], e[0:PAIR, width:])
            for by in range(1, 4):
                chip = jnp.bitwise_and(place[1] - by, 3)
                for side in range(2):
                    part = near[chip, ROWS : 2 * ROWS, pl.ds(side * HALF + i * 256, 256)]
                    total = total + t_dot(part, e[pl.ds(by * PAIR + side * ROWS, ROWS), width:])
            total = total.astype(BF16)
            for j in range(4):
                for side in range(2):
                    out[side, 4 * i + j, 0:64, width:] = total[
                        j * 64 : j * 64 + 64, side * 128 : side * 128 + 128
                    ]
    if kind == "mixer":
        for yl in range(2):
            out[yl, :, 64:80, :] = extra[...]


def weight_grads(kind, place, normed, grads, branch=(), hidden=None, shared=None, extra=None):
    width = {"mixer": 256, "heads": 512, "feed": 768, "lower": 768}[kind]
    every = {"mixer": 256, "heads": 640, "feed": 768, "lower": 768}[kind]
    rows = 80 if kind == "mixer" else 64
    arrays, specs = [], []
    for group in (normed, branch):
        if len(group) == 2:
            arrays += group
            specs += [VMEM, VMEM]
        elif group:
            mine, near, near_at, far, far_at = group
            height = near.shape[1] if kind == "heads" else ROWS
            block = pl.BlockSpec((4, height, D), lambda i, n=near_at: (0, n, 0))
            other = pl.BlockSpec((4, ROWS, D), lambda i, n=far_at: (0, n, 0))
            arrays += [mine, near, far]
            specs += [VMEM, block, other]
    for value in (hidden, shared):
        if value is not None:
            arrays.append(value)
            whole = value is hidden
            specs.append(VMEM if whole else pl.BlockSpec((4, PAIR, D), lambda i: (0, 0, 0)))
    more = list(grads) + ([] if extra is None else [extra])
    return pl.pallas_call(
        functools.partial(weight_grad_kernel, kind),
        grid=(1,),
        out_shape=jax.ShapeDtypeStruct((2, 8, rows, width), BF16),
        in_specs=[SMEM] + specs + [VMEM] * len(more),
        out_specs=VMEM,
        scratch_shapes=[
            pltpu.VMEM((4 * PAIR, D), BF16),
            pltpu.VMEM((4 * PAIR, every), BF16),
        ],
        compiler_params=BIG,
        name="weight_grads",
    )(place, *arrays, *more)


def reduce_rows(packed):
    return lax.all_to_all(packed.reshape((16,) + packed.shape[2:]), SUMS, 0, 0, tiled=True)


def summed(parts):
    return jnp.sum(parts.astype(F32), axis=0).astype(BF16)


def each_part():
    return [(yl, x, c) for yl in range(2) for x in range(4) for c in range(2)]


def feed_out_kernel(first, done, gate, up, down):
    for yl in range(2):
        rows = pl.ds(yl * 64, 64)
        for c in range(2):
            for start, ref in ((0, gate), (256, up)):
                for g in range(2):
                    parts = [
                        done[yl * 8 + x * 2 + c, :, pl.ds(first + start + g * 128, 128)].astype(F32)
                        for x in range(4)
                    ]
                    for i in range(4):
                        out = None
                        for x in range(4):
                            piece = pltpu.roll(parts[x], (x - i) % 4 * 32, 1)
                            keep = in_lanes(piece.shape, x, 32)
                            out = piece if out is None else jnp.where(keep, piece, out)
                        ref[rows, pl.ds((4 * g + i) * 256 + c * 128, 128)] = out
    for i, (yl, x, c) in enumerate(each_part()):
        if first:
            rows = pl.ds(c * 128 + yl * 64, 64)
            down[rows, pl.ds(x * 256, 256)] = done[i, :, first + 512 : first + 768].astype(F32)
            continue
        for k in range(4):
            down[pl.ds(c * 128 + x * 32 + yl * 16, 16), pl.ds(k * 256, 256)] = done[
                i, pl.ds(16 * k, 16), 512:768
            ].astype(F32)


def head_out_kernel(done, q, k, v, out):
    low = in_lanes((64, 128), 0, 64)
    for i, (yl, x, c) in enumerate(each_part()):
        cols = pl.ds(x * 256 + yl * 128, 128)
        out[pl.ds(c * 64, 64), cols] = done[i, :, 1152:1280].astype(F32)
        if c == 1:
            continue
        rows = pl.ds(yl * 64, 64)
        for n, ref in enumerate((q, k, v)):
            lanes = pl.ds(768 + n * 128, 128)
            a, b = done[i, :, lanes].astype(F32), done[i + 1, :, lanes].astype(F32)
            ref[rows, pl.ds(x * 256, 128)] = jnp.where(low, a, pltpu.roll(b, 64, 1))
            ref[rows, pl.ds(x * 256 + 128, 128)] = jnp.where(low, pltpu.roll(a, 64, 1), b)


def mixer_out_kernel(done, first, second, small):
    total = None
    for i, (yl, x, c) in enumerate(each_part()):
        rows, cols = pl.ds(yl * 64, 64), pl.ds(c * HALF + x * 128, 128)
        first[rows, cols] = done[i, 0:64, 0:128].astype(F32)
        second[rows, cols] = done[i, 0:64, 128:256].astype(F32)
        if yl == 0:
            piece = done[i, 64:80, 0:128].astype(F32)
            total = piece if total is None else total + piece
    small[...] = total


def finish(kernel, done, shapes):
    return pl.pallas_call(
        kernel,
        out_shape=[jax.ShapeDtypeStruct(s, F32) for s in shapes],
        in_specs=[VMEM],
        out_specs=[VMEM] * len(shapes),
        compiler_params=BIG,
        name="finish",
    )(done)


def body(
    inputs,
    cotangent,
    lengths,
    mixer_gain,
    mixer_input,
    mixer_gate,
    mixer_kernel,
    lower_gain,
    lower_gate,
    lower_up,
    lower_down,
    attention_gain,
    attention_query,
    attention_key,
    attention_value,
    attention_output,
    upper_gain,
    upper_gate,
    upper_up,
    upper_down,
):
    c, x, yl, yh, z = at("c"), at("x"), at("yl"), at("yh"), at("z")
    chip = yl * 4 + x
    first_chip = (chip == 0).astype(jnp.int32).reshape(1)
    zs = [jnp.mod(z - (1 - 2 * c) * s, 4) for s in range(4)]
    place = jnp.stack([yh * 4 + v for v in zs] + [(1 - yh) * 4 + v for v in zs] + [yl]).astype(
        jnp.int32
    )
    where = jnp.stack([c, x]).astype(jnp.int32)

    small = jnp.concatenate(
        [
            mixer_gain[None],
            lower_gain[None],
            attention_gain[None],
            upper_gain[None],
            mixer_kernel,
            jnp.zeros((9, ROWS), BF16),
        ],
        axis=0,
    )
    upper_part = build(
        upper_part_kernel,
        ((8, 96, D), BF16),
        where,
        upper_gate,
        upper_up,
        upper_down,
        name="upper_part",
    )
    upper_part = lax.all_to_all(upper_part, ("yh", "z"), 0, 0, tiled=True)
    first_slab = build(
        first_slab_kernel,
        ((2, 272, D), BF16),
        where,
        mixer_input,
        mixer_gate,
        small,
        lower_gate,
        lower_up,
        lower_down,
        name="first_slab",
    )
    head_slab = build(
        head_slab_kernel,
        ((2, 128, D), BF16),
        where,
        attention_query,
        attention_key,
        attention_value,
        attention_output,
        name="head_slab",
    )
    pieces, upper_part = gather_slabs([first_slab, head_slab], upper_part)
    upper_pieces = lax.all_gather(upper_part, "x", axis=0, tiled=False)

    mine = jnp.concatenate([inputs[0], cotangent[0]], axis=1)
    two = both_cores(mine, swap_core(mine))
    start = two[:, :D].astype(F32)
    place_row = chip * PAIR + jnp.arange(PAIR, dtype=jnp.int32)
    valid = (place_row < lengths[0]).astype(F32)
    e4 = two[:, D:].astype(F32) * valid[:, None]
    halo = chip_shift(two[PAIR - 16 :, :D], 1)

    mix_w, small_all, lower_in, lower_out = assemble(
        pieces[0],
        FIRST_PLAN,
        [(8, 128, D), (8, 32, 128), (8, 128, 2 * D), (4, 8, 32, D)],
        place,
    )
    mix_w = mix_w.reshape(D, D)
    lower_w = (lower_in.reshape(D, 2 * D), lower_out.reshape(D, D))
    small_all = small_all[:, :16].transpose(1, 0, 2).reshape(16, D).astype(F32)
    gain_m, gain_l, gain_a, gain_u = (small_all[i] for i in range(4))
    taps = lax.dynamic_slice_in_dim(small_all[4:7], c * HALF, HALF, 1)

    with_halo = jnp.concatenate([halo.astype(F32), start], axis=0)
    na_ext, _ = normalize(with_halo, gain_m)
    na = na_ext[16:]
    scale_a = lax.rsqrt(jnp.mean(start * start, axis=-1, keepdims=True) + EPSILON)
    both = dot(na_ext, mix_w)
    signal = both[:, :HALF].astype(BF16).astype(F32)
    gate = both[16:, HALF:]
    shifted = [signal[16:], signal[15:-1], signal[14:-2]]
    conv = sum(taps[m] * shifted[m] for m in range(3))
    mixed = conv * gate
    h1 = start + both_cores(mixed, swap_core(mixed.astype(BF16)).astype(F32), axis=1)

    def feed(stream, gain, weights):
        w_in, w_out = weights
        normed, scale = normalize(stream, gain)
        act = dot(normed, w_in)
        hidden = (jax.nn.silu(act[:, :D]) * act[:, D:]).astype(BF16)
        return normed, scale, act, hidden, dot(hidden, w_out)

    nb, scale_b, act_l, ha, part = feed(h1, gain_l, lower_w)
    h2 = h1 + add_cores(part)
    branch_u = e4.astype(BF16)
    near_1 = from_chips(ha, own_rows(branch_u), own_rows(nb), own_rows(na))

    qkv_w, out_w = assemble(pieces[1], HEAD_PLAN, [(8, 128, 3 * HALF), (8, 64, D)], place)
    qkv_w = qkv_w.reshape(D, 3 * HALF)
    out_w = out_w.reshape(HALF, D)
    nc, scale_c = normalize(h2, gain_a)
    qkv = dot(nc, qkv_w).astype(BF16)
    q = qkv[:, :HALF]
    edge = chip_shift(qkv[PAIR - REACH :, HALF:], 1)
    kv_ext = jnp.concatenate([edge, qkv[:, HALF:]], axis=0)
    k_ext, v_ext = kv_ext[:, :HALF], kv_ext[:, HALF:]
    o = attend(first_chip, q, k_ext, v_ext)
    near_2 = from_chips(own_rows(nc), jnp.concatenate([o[:ROWS], o[ROWS:]], axis=1))
    h3 = h2 + add_cores(dot(o, out_w))

    upper_in, upper_out = pl.pallas_call(
        upper_kernel,
        out_shape=[
            jax.ShapeDtypeStruct((8, 128, 2 * D), BF16),
            jax.ShapeDtypeStruct((4, 8, 32, D), BF16),
        ],
        in_specs=[VMEM],
        out_specs=[VMEM] * 2,
        compiler_params=BIG,
        name="upper_weights",
    )(upper_pieces)
    upper_w = (upper_in.reshape(D, 2 * D), upper_out.reshape(D, D))
    nd, scale_d, act_u, hb, part = feed(h3, gain_u, upper_w)
    other_part = lax.dynamic_slice_in_dim(part, (1 - c) * ROWS, ROWS, 0).astype(BF16)
    outputs = own_rows(h3) + own_rows(part) + swap_core(other_part).astype(F32)

    def feed_back(upper, weights, act, third, normed, branch):
        out = build(
            functools.partial(feed_back_kernel, upper),
            [((PAIR, D), F32)] + [((PAIR, 1280 if upper else 768), BF16)] * 4,
            where,
            act,
            third,
            normed,
            branch,
            *weights,
            name="feed_back",
        )
        return out[0], share_grads(out[1:])

    def from_other_core(grads, first):
        return swap_core(jnp.stack([g[:, first : first + HALF] for g in grads[1:]]))

    partial, grads_u = feed_back(True, upper_w, act_u, hb, nd, branch_u)
    grad_stream, gain_grad_u = norm_back(h3, scale_d, gain_u, add_cores(partial))
    e3 = e4 + grad_stream
    eo = e3.astype(BF16)
    ep = dot_t(eo, out_w).astype(BF16)
    eq, ek_ext, ev_ext = attend_back(first_chip, q, k_ext, v_ext, ep)
    eq, ek_ext, ev_ext, near_1, *grads_u = tie([eq, ek_ext, ev_ext, near_1, *grads_u], [])
    ekv_edge = jnp.concatenate([ek_ext[:REACH], ev_ext[:REACH]], axis=1).astype(BF16)
    back = chip_shift(ekv_edge, -1)
    far_1 = swap_core(near_1[:, PAIR:])
    packed = weight_grads(
        "feed",
        where,
        (nd, from_other_core(grads_u, 768)),
        grads_u,
        (branch_u, near_1, 2, far_1, 0),
    )
    back, packed = tie([back, packed], [])
    sum_u = reduce_rows(packed)
    eqkv, *quarters = build(
        head_pack_kernel,
        [((PAIR, 3 * HALF), BF16)] + [((PAIR, 640), BF16)] * 4,
        where,
        eq,
        ek_ext,
        ev_ext,
        back,
        eo,
        name="head_pack",
    )

    grads_a = share_grads(quarters)
    grad_nc = add_cores(dot_t(eqkv, qkv_w))
    grad_stream, gain_grad_a = norm_back(h2, scale_c, gain_a, grad_nc)
    e2 = e3 + grad_stream
    branch_l = e2.astype(BF16)
    partial, grads_l = feed_back(False, lower_w, act_l, branch_l, nb, branch_l)
    partial, sum_u, near_2, *grads_a = tie([partial, sum_u, near_2, *grads_a], [])
    far_2 = swap_core(near_2[:, :ROWS])

    packed = weight_grads(
        "heads", where, (nc, near_2, 0, far_2, 0), grads_a, hidden=o
    )
    partial, packed = tie([partial, packed], [])
    sum_a = reduce_rows(packed)
    total_u = summed(sum_u)
    grad_stream, gain_grad_l = norm_back(h1, scale_b, gain_l, add_cores(partial))
    e1 = e2 + grad_stream
    e1, total_u, *grads_l = tie([e1, total_u, *grads_l], [])
    packed = weight_grads(
        "lower", where, (nb, near_1, 3, far_1, 1), grads_l, hidden=ha, shared=near_1
    )
    e1, packed = tie([e1, packed], [])
    sum_l = reduce_rows(packed)
    e1_own = lax.dynamic_slice_in_dim(e1, c * HALF, HALF, 1)
    ec = e1_own * gate
    tap_grads = jnp.stack([jnp.sum(ec * shifted[m], axis=0) for m in range(3)])
    ec_next = chip_shift(ec[:8], -1)
    emix, *quarters = pl.pallas_call(
        mixer_pack_kernel,
        out_shape=[jax.ShapeDtypeStruct((PAIR, D), BF16)]
        + [jax.ShapeDtypeStruct((PAIR, 256), BF16)] * 4,
        in_specs=[SMEM] + [VMEM] * 5,
        out_specs=[VMEM] * 5,
        scratch_shapes=[pltpu.VMEM((PAIR + 8, HALF), F32)],
        compiler_params=BIG,
        name="mixer_pack",
    )(where, e1_own, conv, gate, ec_next, jnp.pad(taps, ((0, 5), (0, 0))))
    emix, sum_a, *quarters = tie([emix, sum_a, *quarters], [])

    grads_m = share_grads(quarters)
    total_a = summed(sum_a)
    grad_na = dot_t(emix, mix_w)
    other_na = lax.dynamic_slice_in_dim(grad_na, (1 - c) * ROWS, ROWS, 0).astype(BF16)
    grad_na = own_rows(grad_na) + swap_core(other_na).astype(F32)
    grad_start, gain_grad_m = norm_back(own_rows(start), own_rows(scale_a), gain_m, grad_na)
    input_grad = own_rows(e1) + grad_start
    once = (c == 0).astype(F32)
    wide_taps = lax.dynamic_update_slice(jnp.zeros((3, D), F32), tap_grads, (0, c * HALF))
    gains = jnp.stack([gain_grad_m, gain_grad_l * once, gain_grad_a * once, gain_grad_u * once])
    extra = jnp.concatenate([gains, wide_taps], axis=0).reshape(7, 8, ROWS).transpose(1, 0, 2)
    extra = jnp.pad(extra.astype(BF16), ((0, 0), (0, 9), (0, ROWS)))
    extra, sum_l, total_a, *grads_m = tie([extra, sum_l, total_a, *grads_m], [])
    total = jnp.concatenate([total_u, total_a, summed(sum_l)], axis=1)
    total, *grads_m = tie([total, *grads_m], [])
    done = lax.all_gather(total, SEQ, axis=0, tiled=False)

    packed = weight_grads(
        "mixer", where, (na, near_1, 4, far_1, 2), grads_m, extra=extra
    )
    sum_m = reduce_rows(packed)
    done_m = spread(summed(sum_m), SEQ, 16)
    feed_shapes = [(ROWS, 2 * D), (ROWS, 2 * D), (2 * ROWS, D)]
    upper_grads = finish(functools.partial(feed_out_kernel, 0), done, feed_shapes)
    head_grads = finish(head_out_kernel, done, [(ROWS, D)] * 4)
    lower_grads = finish(functools.partial(feed_out_kernel, 1280), done, feed_shapes)
    in_grad, gate_grad, tail = finish(
        mixer_out_kernel, done_m, [(ROWS, D), (ROWS, D), (16, ROWS)]
    )
    return (
        outputs.astype(BF16)[None],
        input_grad[None],
        tail[0],
        in_grad,
        gate_grad,
        tail[4:7],
        tail[1],
        *lower_grads,
        tail[2],
        *head_grads,
        tail[3],
        *upper_grads,
    )


def solution(mesh):
    fine = Mesh(mesh.devices.reshape(SIZES), AXES)
    rows = ("yh", "z")
    slots = P(rows, SEQ, None)
    vector, matrix, columns = P(rows), P(rows, None), P(None, rows)
    weights = (
        (vector, matrix, matrix, columns)
        + (vector, matrix, matrix, matrix)
        + (vector, matrix, matrix, matrix, matrix)
        + (vector, matrix, matrix, matrix)
    )
    return jax.shard_map(
        body,
        mesh=fine,
        in_specs=(slots, slots, vector) + weights,
        out_specs=(slots, slots) + weights,
        check_vma=False,
    )
```

```python
import functools

import jax
import jax.numpy as jnp
from jax import lax
from jax.experimental import pallas as pl
from jax.experimental.pallas import tpu as pltpu
from jax.sharding import Mesh
from jax.sharding import PartitionSpec as P

EPSILON = 1e-05
MASKED = -1e30
AXES = ("yl", "x", "c", "yh", "z")
SIZES = (2, 4, 2, 2, 4)
SEQ = ("yl", "x", "c")
SUMS = ("yl", "yh", "z")
F32 = jnp.float32
BF16 = jnp.bfloat16
ROWS = 128
PAIR = 256
D = 1024
HALF = 512
REACH = 64
SCALE = 64 ** (-0.5)


def at(axis):
    return lax.axis_index(axis)


def swap_core(value):
    return lax.ppermute(value, "c", [(0, 1), (1, 0)])


def hop_z(value):
    pairs = [(c * 4 + z, c * 4 + (z + 1 - 2 * c) % 4) for c in range(2) for z in range(4)]
    return lax.ppermute(value, ("c", "z"), pairs)


def cross(value):
    return lax.ppermute(value, ("yl", "yh"), [(0, 3), (3, 0), (1, 2), (2, 1)])


def swap_yl(value):
    return lax.ppermute(value, "yl", [(0, 1), (1, 0)])


def chip_shift(value, by):
    pairs = [(i, i + by) for i in range(8) if 0 <= i + by < 8]
    return lax.ppermute(value, ("yl", "x"), pairs)


def along_x(value, by):
    return lax.ppermute(value, "x", [(i, (i + by) % 4) for i in range(4)])


def spread(value, axes, count):
    return lax.all_to_all(
        jnp.broadcast_to(value[None], (count,) + value.shape), axes, 0, 0, tiled=True
    )


def tie(values, after):
    out = lax.optimization_barrier(tuple(values) + tuple(after))
    return out[: len(values)]


def both_cores(own, other, axis=0):
    first = at("c") == 0
    return jnp.concatenate(
        [jnp.where(first, own, other), jnp.where(first, other, own)], axis=axis
    )


VMEM = pl.BlockSpec(memory_space=pltpu.VMEM)
SMEM = pl.BlockSpec(memory_space=pltpu.SMEM)
BIG = pltpu.CompilerParams(vmem_limit_bytes=32 * 1024 * 1024)


def in_lanes(shape, which, width):
    return lax.broadcasted_iota(jnp.int32, shape, 1) // width == which


def hidden_blocks(ref, rows, core):
    blocks = [
        ref[rows, pl.ds(pl.multiple_of(f * 256 + core * 128, 128), 128)].astype(F32)
        for f in range(8)
    ]
    for b in range(8):
        out = None
        for i in range(4):
            source = blocks[4 * (b % 2) + i]
            piece = pltpu.roll(source, (i - b // 2) % 4 * 32, 1)
            out = piece if out is None else jnp.where(in_lanes(piece.shape, i, 32), piece, out)
        yield b, out.astype(BF16)


def head_block(ref, rows, block, core):
    left = ref[rows, pl.ds(block * 256, 128)].astype(F32)
    right = ref[rows, pl.ds(block * 256 + 128, 128)].astype(F32)
    low = lax.broadcasted_iota(jnp.int32, left.shape, 1) < 64
    first = jnp.where(low, left, pltpu.roll(right, 64, 1))
    second = jnp.where(low, pltpu.roll(left, 64, 1), right)
    return jnp.where(core == 0, first, second).astype(BF16)


def first_slab_kernel(place, m_in, m_gate, small, gate, up, down, out):
    core = place[0]
    for half in range(2):
        rows = pl.ds(half * 64, 64)
        for i, ref in enumerate((m_in, m_gate)):
            out[half, 0:64, pl.ds(i * HALF, HALF)] = ref[
                rows, pl.ds(pl.multiple_of(core * HALF, HALF), HALF)
            ]
        out[half, 64:80, :] = jnp.zeros((16, D), BF16)
        out[half, 64:80, 0:128] = small[...]
        for start, ref in ((80, gate), (144, up)):
            for block, value in hidden_blocks(ref, rows, core):
                out[half, pl.ds(start, 64), pl.ds(block * 128, 128)] = value
        out[half, 208:272, :] = down[pl.ds(pl.multiple_of(core * 128 + half * 64, 64), 64), :]


def head_slab_kernel(place, q, k, v, wo, out):
    core = place[0]
    for half in range(2):
        rows = pl.ds(half * 64, 64)
        for block in range(4):
            out[half, 0:64, pl.ds(block * 128, 128)] = head_block(q, rows, block, core)
            out[half, 0:64, pl.ds(512 + block * 128, 128)] = head_block(k, rows, block, core)
            out[half, 64:128, pl.ds(block * 128, 128)] = head_block(v, rows, block, core)
        out[half, 64:128, 512:1024] = wo[
            pl.ds(pl.multiple_of(core * 64, 64), 64), pl.ds(half * HALF, HALF)
        ]


def upper_part_kernel(place, gate, up, down, out):
    core, part = place[0], place[1]
    rows = pl.ds(pl.multiple_of(part * 32, 32), 32)
    low = down[pl.ds(pl.multiple_of(core * 128 + part * 32, 32), 32), :]
    for copy in range(8):
        out[copy, 64:96, :] = low
    for start, ref in ((0, gate), (32, up)):
        for block, value in hidden_blocks(ref, rows, core):
            for copy in range(8):
                out[copy, pl.ds(start, 32), pl.ds(block * 128, 128)] = value


def build(kernel, shapes, place, *arrays, name):
    many = isinstance(shapes, list)
    return pl.pallas_call(
        kernel,
        out_shape=[jax.ShapeDtypeStruct(*s) for s in shapes]
        if many
        else jax.ShapeDtypeStruct(*shapes),
        in_specs=[SMEM] + [VMEM] * len(arrays),
        out_specs=[VMEM] * len(shapes) if many else VMEM,
        compiler_params=BIG,
        name=name,
    )(place, *arrays)


def gather_slabs(slabs, other):
    yl = at("yl")
    state = [dict(own=[s], got=[], rest=[]) for s in slabs]
    moved = []
    for step in range(4 * len(slabs) + 1):
        if moved:
            values = [st[key][-1] for st, key in moved]
            if step == 2:
                *values, other = tie([*values, other], [])
            else:
                values = tie(values, [])
            for (st, key), value in zip(moved, values):
                st[key][-1] = value
        moved, made = [], []
        for g, st in enumerate(state):
            k = step - 4 * g
            if 0 <= k < 3:
                made.append((st, "own", hop_z(st["own"][k])))
            if 1 <= k < 5:
                made.append((st, "rest", swap_yl(st["got"][k - 1])))
            if 0 <= k < 4:
                half = lax.dynamic_index_in_dim(st["own"][k], 1 - yl, 0, keepdims=False)
                made.append((st, "got", cross(half)))
        for st, key, value in made:
            st[key].append(value)
            moved.append((st, key))
    return state, other


def assemble_kernel(plan, place, *refs):
    own, got, rest = refs[0:4], refs[4:8], refs[8:12]
    outs = refs[12:]

    def put(source, f, half):
        for rows, cols, out, height, dest in plan:
            if height == 0:
                for i in range(2):
                    outs[out][half * 2 + i, f] = source[rows.start + i * 32 : rows.start + i * 32 + 32]
                continue
            size = height or HALF
            start = half * size if isinstance(half, int) else pl.multiple_of(half * size, size)
            if height is None:
                outs[out][f, :, pl.ds(start, size)] = source[rows, cols]
            else:
                outs[out][f, pl.ds(start, size), dest] = source[rows, cols]

    yl = place[8]
    for s in range(4):
        for half in range(2):
            put(own[s].at[half], place[s], half)
        put(got[s], place[4 + s], yl)
        put(rest[s], place[4 + s], 1 - yl)


def assemble(pieces, plan, shapes, place):
    return build(
        functools.partial(assemble_kernel, plan),
        [(s, BF16) for s in shapes],
        place,
        *pieces["own"],
        *pieces["got"],
        *pieces["rest"],
        name="assemble",
    )


ALL = slice(0, D)
FIRST_PLAN = [
    (slice(0, 64), ALL, 0, 64, ALL),
    (slice(64, 80), slice(0, 128), 1, 16, slice(0, 128)),
    (slice(80, 144), ALL, 2, 64, ALL),
    (slice(144, 208), ALL, 2, 64, slice(D, 2 * D)),
    (slice(208, 272), ALL, 3, 0, ALL),
]
HEAD_PLAN = [
    (slice(0, 64), ALL, 0, 64, ALL),
    (slice(64, 128), slice(0, HALF), 0, 64, slice(D, D + HALF)),
    (slice(64, 128), slice(HALF, D), 1, None, None),
]


def upper_kernel(pieces, w_in, w_out):
    for part in range(4):
        rows = pl.ds(part * 32, 32)
        w_in[:, rows, 0:D] = pieces[part, :, 0:32, :]
        w_in[:, rows, D : 2 * D] = pieces[part, :, 32:64, :]
        w_out[part] = pieces[part, :, 64:96, :]


def dot(left, right, dims=((1,), (0,))):
    return lax.dot_general(left, right, (dims, ((), ())), preferred_element_type=F32)


def dot_t(left, right):
    return dot(left, right, ((1,), (1,)))


def t_dot(left, right):
    return dot(left, right, ((0,), (0,)))


def normalize(stream, gain):
    scale = lax.rsqrt(jnp.mean(stream * stream, axis=-1, keepdims=True) + EPSILON)
    return (stream * scale * gain).astype(BF16), scale


def norm_back(stream, scale, gain, upstream):
    weighted = upstream * gain
    inner = jnp.mean(weighted * stream, axis=-1, keepdims=True)
    grad = scale * (weighted - stream * scale * scale * inner)
    return grad, jnp.sum(upstream * stream * scale, axis=0)


def add_cores(partial):
    return partial + swap_core(partial.astype(BF16)).astype(F32)


def lane_mask(shape, head):
    lane = lax.broadcasted_iota(jnp.int32, shape, 1)
    return (lane // 64) == head


def window_mask(block, first):
    i = lax.broadcasted_iota(jnp.int32, (128, 192), 0)
    j = lax.broadcasted_iota(jnp.int32, (128, 192), 1)
    allowed = (j > i) & (j <= i + REACH)
    if block == 0:
        allowed = allowed & ((j >= REACH) | (first == 0))
    return allowed


def probabilities(q, k, allowed):
    scores = jnp.where(allowed, dot_t(q, k) * SCALE, MASKED)
    weights = jnp.exp(scores - jnp.max(scores, axis=-1, keepdims=True))
    return weights / jnp.sum(weights, axis=-1, keepdims=True)


def attend_kernel(first_ref, q_ref, k_ref, v_ref, o_ref):
    for block in range(2):
        allowed = window_mask(block, first_ref[0])
        rows, keys = pl.ds(block * 128, 128), pl.ds(block * 128, 192)
        for pair in range(4):
            cols = pl.ds(pair * 128, 128)
            q, k, v = q_ref[rows, cols], k_ref[keys, cols], v_ref[keys, cols]
            outs = []
            for head in range(2):
                q_head = jnp.where(lane_mask(q.shape, head), q, jnp.zeros_like(q))
                p = probabilities(q_head, k, allowed)
                outs.append(dot(p.astype(BF16), v))
            o_ref[rows, cols] = jnp.where(lane_mask(q.shape, 0), outs[0], outs[1]).astype(BF16)


def attend(first, q, k_ext, v_ext):
    return pl.pallas_call(
        attend_kernel,
        out_shape=jax.ShapeDtypeStruct((PAIR, HALF), BF16),
        in_specs=[pl.BlockSpec(memory_space=pltpu.SMEM)]
        + [pl.BlockSpec(memory_space=pltpu.VMEM)] * 3,
        out_specs=pl.BlockSpec(memory_space=pltpu.VMEM),
        name="attend",
    )(first, q, k_ext, v_ext)


def attend_back_kernel(first_ref, q_ref, k_ref, v_ref, ep_ref, eq_ref, ek_ref, ev_ref):
    for pair in range(4):
        cols = pl.ds(pair * 128, 128)
        eks, evs = [], []
        for block in range(2):
            allowed = window_mask(block, first_ref[0])
            rows, keys = pl.ds(block * 128, 128), pl.ds(block * 128, 192)
            q, k, v = q_ref[rows, cols], k_ref[keys, cols], v_ref[keys, cols]
            ep = ep_ref[rows, cols]
            eq_out, ek_out, ev_out = [], [], []
            for head in range(2):
                own = lane_mask(q.shape, head)
                p = probabilities(jnp.where(own, q, jnp.zeros_like(q)), k, allowed)
                dp = dot_t(jnp.where(own, ep, jnp.zeros_like(ep)), v)
                inner = jnp.sum(p * dp, axis=-1, keepdims=True)
                es = (p * (dp - inner)).astype(BF16)
                ev_out.append(t_dot(p.astype(BF16), ep))
                ek_out.append(t_dot(es, q))
                eq_out.append(dot(es, k))
            pick_q = lane_mask((128, 128), 0)
            pick_k = lane_mask((192, 128), 0)
            eq_ref[rows, cols] = (jnp.where(pick_q, eq_out[0], eq_out[1]) * SCALE).astype(BF16)
            eks.append(jnp.where(pick_k, ek_out[0], ek_out[1]) * SCALE)
            evs.append(jnp.where(pick_k, ev_out[0], ev_out[1]))
        for parts, ref in ((eks, ek_ref), (evs, ev_ref)):
            ref[pl.ds(0, 128), cols] = parts[0][:128]
            ref[pl.ds(128, 64), cols] = parts[0][128:] + parts[1][:64]
            ref[pl.ds(192, 128), cols] = parts[1][64:]


def attend_back(first, q, k_ext, v_ext, ep):
    return pl.pallas_call(
        attend_back_kernel,
        out_shape=[
            jax.ShapeDtypeStruct((PAIR, HALF), BF16),
            jax.ShapeDtypeStruct((PAIR + REACH, HALF), F32),
            jax.ShapeDtypeStruct((PAIR + REACH, HALF), F32),
        ],
        in_specs=[pl.BlockSpec(memory_space=pltpu.SMEM)]
        + [pl.BlockSpec(memory_space=pltpu.VMEM)] * 4,
        out_specs=[pl.BlockSpec(memory_space=pltpu.VMEM)] * 3,
        name="attend_back",
    )(first, q, k_ext, v_ext, ep)


def own_rows(value):
    return lax.dynamic_slice_in_dim(value, at("c") * ROWS, ROWS, 0)


def share_grads(quarters):
    return [quarters[0]] + [along_x(quarters[by], by) for by in range(1, 4)]


def from_chips(*values):
    return lax.all_gather(jnp.concatenate(values, axis=0), "x", axis=0, tiled=False)


def quarter(place, by, width, offset=0):
    start = jnp.bitwise_and(place[1] + by, 3) * width + offset
    return pl.ds(pl.multiple_of(start, 128), width)


def carry_rows(place, out, first, normed):
    rows = pl.ds(pl.multiple_of(place[0] * ROWS, ROWS), ROWS)
    for side in range(2):
        part = normed[rows, pl.ds(side * HALF, HALF)]
        out[pl.ds(side * ROWS, ROWS), pl.ds(first, HALF)] = part


def feed_back_kernel(upper, place, act, third, normed, branch, w_in, w_out, partial, *quarters):
    for by in range(4):
        cols, up_cols = quarter(place, by, 256), quarter(place, by, 256, D)
        grad_hidden = dot_t(branch[...], w_out[cols, :])
        gate_act, up_act = act[:, cols], act[:, up_cols]
        sig = 1.0 / (1.0 + jnp.exp(-gate_act))
        grad_gate = (grad_hidden * up_act * sig * (1.0 + gate_act * (1.0 - sig))).astype(BF16)
        grad_up = (grad_hidden * gate_act * sig).astype(BF16)
        out = quarters[by]
        out[:, 0:256] = grad_gate
        out[:, 256:512] = grad_up
        out[:, 512:768] = third[:, cols]
        if upper:
            carry_rows(place, out, 768, normed)
        piece = dot_t(grad_gate, w_in[:, cols]) + dot_t(grad_up, w_in[:, up_cols])
        if by == 0:
            partial[...] = piece
        else:
            partial[...] += piece


def head_pack_kernel(place, eq, ek_ext, ev_ext, back, eo, eqkv, *quarters):
    cut = PAIR - REACH
    eqkv[:, 0:HALF] = eq[...]
    for i, ref in enumerate((ek_ext, ev_ext)):
        cols = pl.ds((i + 1) * HALF, HALF)
        eqkv[0:cut, cols] = ref[REACH:PAIR, :].astype(BF16)
        tail = ref[PAIR : PAIR + REACH, :] + back[:, pl.ds(i * HALF, HALF)].astype(F32)
        eqkv[cut:PAIR, cols] = tail.astype(BF16)
    for by in range(4):
        for i in range(3):
            quarters[by][:, pl.ds(i * 128, 128)] = eqkv[:, quarter(place, by, 128, i * HALF)]
        quarters[by][:, 384:640] = eo[:, quarter(place, by, 256)]


def mixer_pack_kernel(place, e1, conv, gate, after, taps, emix, *rest):
    quarters, ec = rest[:4], rest[4]
    ec[0:PAIR, :] = e1[...] * gate[...]
    ec[PAIR : PAIR + 8, :] = after[...]
    esig = taps[0:1, :] * ec[0:PAIR, :]
    for m in (1, 2):
        esig = esig + taps[m : m + 1, :] * ec[m : m + PAIR, :]
    emix[:, 0:HALF] = esig.astype(BF16)
    emix[:, HALF:D] = (e1[...] * conv[...]).astype(BF16)
    for by in range(4):
        for i in range(2):
            quarters[by][:, pl.ds(i * 128, 128)] = emix[:, quarter(place, by, 128, i * HALF)]


def fill_rows(place, out, mine, near, far):
    core = place[0]
    out[0:PAIR, :] = mine[...]
    for by in range(1, 4):
        chip = jnp.bitwise_and(place[1] - by, 3)
        for ref, c in ((near, core), (far, 1 - core)):
            rows = pl.ds(pl.multiple_of(by * PAIR + c * ROWS, ROWS), ROWS)
            out[rows, :] = ref[chip, 0:ROWS, :]


def fill_carried(place, out, mine, far, grads, first):
    core = place[0]
    out[0:PAIR, :] = mine[...]
    for by in range(1, 4):
        near_rows = pl.ds(pl.multiple_of(by * PAIR + core * ROWS, ROWS), ROWS)
        far_rows = pl.ds(pl.multiple_of(by * PAIR + (1 - core) * ROWS, ROWS), ROWS)
        for side in range(2):
            rows, cols = pl.ds(side * ROWS, ROWS), pl.ds(side * HALF, HALF)
            out[near_rows, cols] = grads[by][rows, pl.ds(first, HALF)]
            out[far_rows, cols] = far[by - 1, rows, :]


def weight_grad_kernel(kind, place, mine, *rest):
    rest = list(rest)
    near = rest.pop(0) if kind != "feed" else None
    far = rest.pop(0)
    if kind == "feed":
        branch = [rest.pop(0) for _ in range(3)]
    if kind in ("heads", "lower"):
        hidden = rest.pop(0)
    if kind == "lower":
        shared = rest.pop(0)
    grads = [rest.pop(0) for _ in range(4)]
    if kind == "mixer":
        extra = rest.pop(0)
    out, normed, e = rest[:3]
    every = e.shape[1]
    if near is None:
        fill_carried(place, normed, mine, far, grads, every)
    else:
        fill_rows(place, normed, mine, near, far)
    for by in range(4):
        e[pl.ds(by * PAIR, PAIR), :] = grads[by][:, 0:every]
    width = {"mixer": 256, "heads": 384, "feed": 512, "lower": 512}[kind]
    for i in range(4):
        got = t_dot(normed[:, pl.ds(i * 256, 256)], e[:, 0:width]).astype(BF16)
        for j in range(4):
            out[j % 2, 2 * i + j // 2, 0:64, 0:width] = got[j * 64 : j * 64 + 64]
    if kind == "feed":
        fill_rows(place, normed, *branch)
        for k in range(4):
            got = t_dot(e[:, width:], normed[:, pl.ds(k * 256, 256)]).astype(BF16)
            for f in range(8):
                for yl in range(2):
                    out[yl, f, pl.ds(16 * k, 16), width:] = got[f * 32 + yl * 16 : f * 32 + yl * 16 + 16]
    if kind == "lower":
        for i in range(4):
            cols = pl.ds(i * 256, 256)
            total = t_dot(hidden[:, cols], e[0:PAIR, width:])
            for by in range(1, 4):
                chip = jnp.bitwise_and(place[1] - by, 3)
                total = total + t_dot(shared[chip, :, cols], e[pl.ds(by * PAIR, PAIR), width:])
            total = total.astype(BF16)
            for f in range(8):
                out[i // 2, f, pl.ds(i % 2 * 32, 32), width:] = total[f * 32 : f * 32 + 32]
    if kind == "heads":
        for i in range(2):
            total = t_dot(hidden[:, pl.ds(i * 256, 256)], e[0:PAIR, width:])
            for by in range(1, 4):
                chip = jnp.bitwise_and(place[1] - by, 3)
                for side in range(2):
                    part = near[chip, ROWS : 2 * ROWS, pl.ds(side * HALF + i * 256, 256)]
                    total = total + t_dot(part, e[pl.ds(by * PAIR + side * ROWS, ROWS), width:])
            total = total.astype(BF16)
            for j in range(4):
                for side in range(2):
                    out[side, 4 * i + j, 0:64, width:] = total[
                        j * 64 : j * 64 + 64, side * 128 : side * 128 + 128
                    ]
    if kind == "mixer":
        for yl in range(2):
            out[yl, :, 64:80, :] = extra[...]


def weight_grads(kind, place, normed, grads, branch=(), hidden=None, shared=None, extra=None):
    width = {"mixer": 256, "heads": 512, "feed": 768, "lower": 768}[kind]
    every = {"mixer": 256, "heads": 640, "feed": 768, "lower": 768}[kind]
    rows = 80 if kind == "mixer" else 64
    arrays, specs = [], []
    for group in (normed, branch):
        if len(group) == 2:
            arrays += group
            specs += [VMEM, VMEM]
        elif group:
            mine, near, near_at, far, far_at = group
            height = near.shape[1] if kind == "heads" else ROWS
            block = pl.BlockSpec((4, height, D), lambda i, n=near_at: (0, n, 0))
            other = pl.BlockSpec((4, ROWS, D), lambda i, n=far_at: (0, n, 0))
            arrays += [mine, near, far]
            specs += [VMEM, block, other]
    for value in (hidden, shared):
        if value is not None:
            arrays.append(value)
            whole = value is hidden
            specs.append(VMEM if whole else pl.BlockSpec((4, PAIR, D), lambda i: (0, 0, 0)))
    more = list(grads) + ([] if extra is None else [extra])
    return pl.pallas_call(
        functools.partial(weight_grad_kernel, kind),
        grid=(1,),
        out_shape=jax.ShapeDtypeStruct((2, 8, rows, width), BF16),
        in_specs=[SMEM] + specs + [VMEM] * len(more),
        out_specs=VMEM,
        scratch_shapes=[
            pltpu.VMEM((4 * PAIR, D), BF16),
            pltpu.VMEM((4 * PAIR, every), BF16),
        ],
        compiler_params=BIG,
        name="weight_grads",
    )(place, *arrays, *more)


def reduce_rows(packed):
    return lax.all_to_all(packed.reshape((16,) + packed.shape[2:]), SUMS, 0, 0, tiled=True)


def summed(parts):
    return jnp.sum(parts.astype(F32), axis=0).astype(BF16)


def each_part():
    return [(yl, x, c) for yl in range(2) for x in range(4) for c in range(2)]


def put_columns(done, start, ref, c):
    for g in range(2):
        parts = [
            done[x * 2 + c, :, pl.ds(start + g * 128, 128)].astype(F32) for x in range(4)
        ]
        for i in range(4):
            out = None
            for x in range(4):
                piece = pltpu.roll(parts[x], (x - i) % 4 * 32, 1)
                keep = in_lanes(piece.shape, x, 32)
                out = piece if out is None else jnp.where(keep, piece, out)
            ref[:, pl.ds((4 * g + i) * 256 + c * 128, 128)] = out


def layers_out_kernel(done, gate_u, up_u, down_u, q, k, v, out, gate_l, up_l, down_l):
    yl = pl.program_id(0)
    low = in_lanes((64, 128), 0, 64)
    for c in range(2):
        put_columns(done, 0, gate_u, c)
        put_columns(done, 256, up_u, c)
        put_columns(done, 1280, gate_l, c)
        put_columns(done, 1536, up_l, c)
        for x in range(4):
            part = done.at[x * 2 + c]
            for k4 in range(4):
                rows = pl.ds(pl.multiple_of(c * 128 + x * 32 + yl * 16, 16), 16)
                down_u[rows, pl.ds(k4 * 256, 256)] = part[pl.ds(16 * k4, 16), 512:768].astype(F32)
            rows = pl.ds(pl.multiple_of(c * 128 + yl * 64, 64), 64)
            down_l[rows, pl.ds(x * 256, 256)] = part[:, 1792:2048].astype(F32)
            cols = pl.ds(pl.multiple_of(x * 256 + yl * 128, 128), 128)
            out[pl.ds(c * 64, 64), cols] = part[:, 1152:1280].astype(F32)
    for x in range(4):
        for n, ref in enumerate((q, k, v)):
            lanes = pl.ds(768 + n * 128, 128)
            a, b = done[x * 2, :, lanes].astype(F32), done[x * 2 + 1, :, lanes].astype(F32)
            ref[:, pl.ds(x * 256, 128)] = jnp.where(low, a, pltpu.roll(b, 64, 1))
            ref[:, pl.ds(x * 256 + 128, 128)] = jnp.where(low, pltpu.roll(a, 64, 1), b)


def layers_out(done):
    shapes = [(ROWS, 2 * D), (ROWS, 2 * D), (2 * ROWS, D)]
    shapes = shapes + [(ROWS, D)] * 4 + shapes
    by_yl = [True, True, False, True, True, True, False, True, True, False]
    specs = [
        pl.BlockSpec((64, n), lambda i: (i, 0)) if cut else pl.BlockSpec((m, n), lambda i: (0, 0))
        for (m, n), cut in zip(shapes, by_yl)
    ]
    return pl.pallas_call(
        layers_out_kernel,
        grid=(2,),
        out_shape=[jax.ShapeDtypeStruct(shape, F32) for shape in shapes],
        in_specs=[pl.BlockSpec((8, 64, 4 * HALF), lambda i: (i, 0, 0))],
        out_specs=specs,
        compiler_params=BIG,
        name="layers_out",
    )(done)


def mixer_out_kernel(done, first, second, small):
    total = None
    for i, (yl, x, c) in enumerate(each_part()):
        rows, cols = pl.ds(yl * 64, 64), pl.ds(c * HALF + x * 128, 128)
        first[rows, cols] = done[i, 0:64, 0:128].astype(F32)
        second[rows, cols] = done[i, 0:64, 128:256].astype(F32)
        if yl == 0:
            piece = done[i, 64:80, 0:128].astype(F32)
            total = piece if total is None else total + piece
    small[...] = total


def finish(kernel, done, shapes):
    return pl.pallas_call(
        kernel,
        out_shape=[jax.ShapeDtypeStruct(s, F32) for s in shapes],
        in_specs=[VMEM],
        out_specs=[VMEM] * len(shapes),
        compiler_params=BIG,
        name="finish",
    )(done)


def body(
    inputs,
    cotangent,
    lengths,
    mixer_gain,
    mixer_input,
    mixer_gate,
    mixer_kernel,
    lower_gain,
    lower_gate,
    lower_up,
    lower_down,
    attention_gain,
    attention_query,
    attention_key,
    attention_value,
    attention_output,
    upper_gain,
    upper_gate,
    upper_up,
    upper_down,
):
    c, x, yl, yh, z = at("c"), at("x"), at("yl"), at("yh"), at("z")
    chip = yl * 4 + x
    first_chip = (chip == 0).astype(jnp.int32).reshape(1)
    zs = [jnp.mod(z - (1 - 2 * c) * s, 4) for s in range(4)]
    place = jnp.stack([yh * 4 + v for v in zs] + [(1 - yh) * 4 + v for v in zs] + [yl]).astype(
        jnp.int32
    )
    where = jnp.stack([c, x]).astype(jnp.int32)

    small = jnp.concatenate(
        [
            mixer_gain[None],
            lower_gain[None],
            attention_gain[None],
            upper_gain[None],
            mixer_kernel,
            jnp.zeros((9, ROWS), BF16),
        ],
        axis=0,
    )
    upper_part = build(
        upper_part_kernel,
        ((8, 96, D), BF16),
        where,
        upper_gate,
        upper_up,
        upper_down,
        name="upper_part",
    )
    upper_part = lax.all_to_all(upper_part, ("yh", "z"), 0, 0, tiled=True)
    first_slab = build(
        first_slab_kernel,
        ((2, 272, D), BF16),
        where,
        mixer_input,
        mixer_gate,
        small,
        lower_gate,
        lower_up,
        lower_down,
        name="first_slab",
    )
    head_slab = build(
        head_slab_kernel,
        ((2, 128, D), BF16),
        where,
        attention_query,
        attention_key,
        attention_value,
        attention_output,
        name="head_slab",
    )
    pieces, upper_part = gather_slabs([first_slab, head_slab], upper_part)
    upper_pieces = lax.all_gather(upper_part, "x", axis=0, tiled=False)

    mine = jnp.concatenate([inputs[0], cotangent[0]], axis=1)
    two = both_cores(mine, swap_core(mine))
    start = two[:, :D].astype(F32)
    place_row = chip * PAIR + jnp.arange(PAIR, dtype=jnp.int32)
    valid = (place_row < lengths[0]).astype(F32)
    e4 = two[:, D:].astype(F32) * valid[:, None]
    halo = chip_shift(two[PAIR - 16 :, :D], 1)

    mix_w, small_all, lower_in, lower_out = assemble(
        pieces[0],
        FIRST_PLAN,
        [(8, 128, D), (8, 32, 128), (8, 128, 2 * D), (4, 8, 32, D)],
        place,
    )
    mix_w = mix_w.reshape(D, D)
    lower_w = (lower_in.reshape(D, 2 * D), lower_out.reshape(D, D))
    small_all = small_all[:, :16].transpose(1, 0, 2).reshape(16, D).astype(F32)
    gain_m, gain_l, gain_a, gain_u = (small_all[i] for i in range(4))
    taps = lax.dynamic_slice_in_dim(small_all[4:7], c * HALF, HALF, 1)

    with_halo = jnp.concatenate([halo.astype(F32), start], axis=0)
    na_ext, _ = normalize(with_halo, gain_m)
    na = na_ext[16:]
    scale_a = lax.rsqrt(jnp.mean(start * start, axis=-1, keepdims=True) + EPSILON)
    both = dot(na_ext, mix_w)
    signal = both[:, :HALF].astype(BF16).astype(F32)
    gate = both[16:, HALF:]
    shifted = [signal[16:], signal[15:-1], signal[14:-2]]
    conv = sum(taps[m] * shifted[m] for m in range(3))
    mixed = conv * gate
    h1 = start + both_cores(mixed, swap_core(mixed.astype(BF16)).astype(F32), axis=1)

    def feed(stream, gain, weights):
        w_in, w_out = weights
        normed, scale = normalize(stream, gain)
        act = dot(normed, w_in)
        hidden = (jax.nn.silu(act[:, :D]) * act[:, D:]).astype(BF16)
        return normed, scale, act, hidden, dot(hidden, w_out)

    nb, scale_b, act_l, ha, part = feed(h1, gain_l, lower_w)
    h2 = h1 + add_cores(part)
    branch_u = e4.astype(BF16)
    near_1 = from_chips(ha, own_rows(branch_u), own_rows(nb), own_rows(na))

    qkv_w, out_w = assemble(pieces[1], HEAD_PLAN, [(8, 128, 3 * HALF), (8, 64, D)], place)
    qkv_w = qkv_w.reshape(D, 3 * HALF)
    out_w = out_w.reshape(HALF, D)
    nc, scale_c = normalize(h2, gain_a)
    qkv = dot(nc, qkv_w).astype(BF16)
    q = qkv[:, :HALF]
    edge = chip_shift(qkv[PAIR - REACH :, HALF:], 1)
    kv_ext = jnp.concatenate([edge, qkv[:, HALF:]], axis=0)
    k_ext, v_ext = kv_ext[:, :HALF], kv_ext[:, HALF:]
    o = attend(first_chip, q, k_ext, v_ext)
    near_2 = from_chips(own_rows(nc), jnp.concatenate([o[:ROWS], o[ROWS:]], axis=1))
    h3 = h2 + add_cores(dot(o, out_w))

    upper_in, upper_out = pl.pallas_call(
        upper_kernel,
        out_shape=[
            jax.ShapeDtypeStruct((8, 128, 2 * D), BF16),
            jax.ShapeDtypeStruct((4, 8, 32, D), BF16),
        ],
        in_specs=[VMEM],
        out_specs=[VMEM] * 2,
        compiler_params=BIG,
        name="upper_weights",
    )(upper_pieces)
    upper_w = (upper_in.reshape(D, 2 * D), upper_out.reshape(D, D))
    nd, scale_d, act_u, hb, part = feed(h3, gain_u, upper_w)
    other_part = lax.dynamic_slice_in_dim(part, (1 - c) * ROWS, ROWS, 0).astype(BF16)
    outputs = own_rows(h3) + own_rows(part) + swap_core(other_part).astype(F32)

    def feed_back(upper, weights, act, third, normed, branch):
        out = build(
            functools.partial(feed_back_kernel, upper),
            [((PAIR, D), F32)] + [((PAIR, 1280 if upper else 768), BF16)] * 4,
            where,
            act,
            third,
            normed,
            branch,
            *weights,
            name="feed_back",
        )
        return out[0], share_grads(out[1:])

    def from_other_core(grads, first):
        return swap_core(jnp.stack([g[:, first : first + HALF] for g in grads[1:]]))

    partial, grads_u = feed_back(True, upper_w, act_u, hb, nd, branch_u)
    grad_stream, gain_grad_u = norm_back(h3, scale_d, gain_u, add_cores(partial))
    e3 = e4 + grad_stream
    eo = e3.astype(BF16)
    ep = dot_t(eo, out_w).astype(BF16)
    eq, ek_ext, ev_ext = attend_back(first_chip, q, k_ext, v_ext, ep)
    eq, ek_ext, ev_ext, near_1, *grads_u = tie([eq, ek_ext, ev_ext, near_1, *grads_u], [])
    ekv_edge = jnp.concatenate([ek_ext[:REACH], ev_ext[:REACH]], axis=1).astype(BF16)
    back = chip_shift(ekv_edge, -1)
    far_1 = swap_core(near_1[:, PAIR:])
    packed = weight_grads(
        "feed",
        where,
        (nd, from_other_core(grads_u, 768)),
        grads_u,
        (branch_u, near_1, 2, far_1, 0),
    )
    back, packed = tie([back, packed], [])
    sum_u = reduce_rows(packed)
    eqkv, *quarters = build(
        head_pack_kernel,
        [((PAIR, 3 * HALF), BF16)] + [((PAIR, 640), BF16)] * 4,
        where,
        eq,
        ek_ext,
        ev_ext,
        back,
        eo,
        name="head_pack",
    )

    grads_a = share_grads(quarters)
    grad_nc = add_cores(dot_t(eqkv, qkv_w))
    grad_stream, gain_grad_a = norm_back(h2, scale_c, gain_a, grad_nc)
    e2 = e3 + grad_stream
    branch_l = e2.astype(BF16)
    partial, grads_l = feed_back(False, lower_w, act_l, branch_l, nb, branch_l)
    partial, sum_u, near_2, *grads_a = tie([partial, sum_u, near_2, *grads_a], [])
    far_2 = swap_core(near_2[:, :ROWS])

    packed = weight_grads(
        "heads", where, (nc, near_2, 0, far_2, 0), grads_a, hidden=o
    )
    partial, packed = tie([partial, packed], [])
    sum_a = reduce_rows(packed)
    total_u = summed(sum_u)
    grad_stream, gain_grad_l = norm_back(h1, scale_b, gain_l, add_cores(partial))
    e1 = e2 + grad_stream
    e1, total_u, *grads_l = tie([e1, total_u, *grads_l], [])
    packed = weight_grads(
        "lower", where, (nb, near_1, 3, far_1, 1), grads_l, hidden=ha, shared=near_1
    )
    e1, packed = tie([e1, packed], [])
    sum_l = reduce_rows(packed)
    e1_own = lax.dynamic_slice_in_dim(e1, c * HALF, HALF, 1)
    ec = e1_own * gate
    tap_grads = jnp.stack([jnp.sum(ec * shifted[m], axis=0) for m in range(3)])
    ec_next = chip_shift(ec[:8], -1)
    emix, *quarters = pl.pallas_call(
        mixer_pack_kernel,
        out_shape=[jax.ShapeDtypeStruct((PAIR, D), BF16)]
        + [jax.ShapeDtypeStruct((PAIR, 256), BF16)] * 4,
        in_specs=[SMEM] + [VMEM] * 5,
        out_specs=[VMEM] * 5,
        scratch_shapes=[pltpu.VMEM((PAIR + 8, HALF), F32)],
        compiler_params=BIG,
        name="mixer_pack",
    )(where, e1_own, conv, gate, ec_next, jnp.pad(taps, ((0, 5), (0, 0))))
    emix, sum_a, *quarters = tie([emix, sum_a, *quarters], [])

    grads_m = share_grads(quarters)
    total_a = summed(sum_a)
    grad_na = dot_t(emix, mix_w)
    other_na = lax.dynamic_slice_in_dim(grad_na, (1 - c) * ROWS, ROWS, 0).astype(BF16)
    grad_na = own_rows(grad_na) + swap_core(other_na).astype(F32)
    grad_start, gain_grad_m = norm_back(own_rows(start), own_rows(scale_a), gain_m, grad_na)
    input_grad = own_rows(e1) + grad_start
    once = (c == 0).astype(F32)
    wide_taps = lax.dynamic_update_slice(jnp.zeros((3, D), F32), tap_grads, (0, c * HALF))
    gains = jnp.stack([gain_grad_m, gain_grad_l * once, gain_grad_a * once, gain_grad_u * once])
    extra = jnp.concatenate([gains, wide_taps], axis=0).reshape(7, 8, ROWS).transpose(1, 0, 2)
    extra = jnp.pad(extra.astype(BF16), ((0, 0), (0, 9), (0, ROWS)))
    extra, sum_l, total_a, *grads_m = tie([extra, sum_l, total_a, *grads_m], [])
    total = jnp.concatenate([total_u, total_a, summed(sum_l)], axis=1)
    total, *grads_m = tie([total, *grads_m], [])
    done = lax.all_gather(total, SEQ, axis=0, tiled=False)

    packed = weight_grads(
        "mixer", where, (na, near_1, 4, far_1, 2), grads_m, extra=extra
    )
    sum_m = reduce_rows(packed)
    done_m = spread(summed(sum_m), SEQ, 16)
    layers = layers_out(done)
    upper_grads, head_grads, lower_grads = layers[:3], layers[3:7], layers[7:]
    in_grad, gate_grad, tail = finish(
        mixer_out_kernel, done_m, [(ROWS, D), (ROWS, D), (16, ROWS)]
    )
    return (
        outputs.astype(BF16)[None],
        input_grad[None],
        tail[0],
        in_grad,
        gate_grad,
        tail[4:7],
        tail[1],
        *lower_grads,
        tail[2],
        *head_grads,
        tail[3],
        *upper_grads,
    )


def solution(mesh):
    fine = Mesh(mesh.devices.reshape(SIZES), AXES)
    rows = ("yh", "z")
    slots = P(rows, SEQ, None)
    vector, matrix, columns = P(rows), P(rows, None), P(None, rows)
    weights = (
        (vector, matrix, matrix, columns)
        + (vector, matrix, matrix, matrix)
        + (vector, matrix, matrix, matrix, matrix)
        + (vector, matrix, matrix, matrix)
    )
    return jax.shard_map(
        body,
        mesh=fine,
        in_specs=(slots, slots, vector) + weights,
        out_specs=(slots, slots) + weights,
        check_vma=False,
    )
```
